32 devices in a mesh: groups: 2 (over y), row: 8 (over z, x), col: 2 (over core).
Axes of the slice: x: 2, y: 2, z: 4, core: 2. Of those that a mesh axis runs over, the one named last changes fastest.
Arguments:
- blocks: bfloat16 [16, 2, 128, 128, 128], P(('groups', 'row'), 'col'), parts along dimension 0, may hold values from -0.09375 to 0.09375
- block_rows: int32 [16, 2, 128], P(('groups', 'row'), 'col'), parts along dimension 0, may hold values from 0 to 7
- block_cols: int32 [16, 2, 128], P(('groups', 'row'), 'col'), parts along dimension 0, may hold values from 0 to 63, as said below
- block_counts: int32 [16, 2], P(('groups', 'row'), 'col'), parts along dimension 0, may hold values from 96 to 128
- primal: float32 [256, 128], P(('groups', 'col', 'row')), parts along dimension 0, may hold values from -3 to 3
- primal_bar: float32 [256, 128], P(('groups', 'col', 'row')), parts along dimension 0, may hold values from -3 to 3
- dual: float32 [128, 128], P(('groups', 'row', 'col')), parts along dimension 0, may hold values from -5 to 5
- rhs: float32 [128, 128], P(('groups', 'row', 'col')), parts along dimension 0, may hold values from -5 to 5
- cost_vec: float32 [256, 128], P(('groups', 'col', 'row')), parts along dimension 0, may hold values from -5 to 5
- lower: float32 [256, 128], P(('groups', 'col', 'row')), parts along dimension 0, may hold values from -1 to -0.1
- upper: float32 [256, 128], P(('groups', 'col', 'row')), parts along dimension 0, may hold values from 0.1 to 1
- bound_kind: int32 [256, 128], P(('groups', 'col', 'row')), parts along dimension 0, may hold values from 0 to 3
- row_kind: int32 [128, 128], P(('groups', 'row', 'col')), parts along dimension 0, may hold values from 0 to 1
- primal_step: float32 [2], P('groups'), parts along dimension 0, may hold values from 0.3 to 1
- dual_step: float32 [2], P('groups'), parts along dimension 0, may hold values from 0.3 to 1
Outputs:
- dual_new: float32 [128, 128], P(('groups', 'row', 'col')), parts along dimension 0
- primal_new: float32 [256, 128], P(('groups', 'col', 'row')), parts along dimension 0
- primal_bar_new: float32 [256, 128], P(('groups', 'col', 'row')), parts along dimension 0
The draws below stay inside these ranges and needn't reach their ends.
There are 2 independent parts, one for each index of `groups`. The reference program is written for one: setup_inputs(seed, part) draws one part's arguments, and reference() takes and returns one part's arrays. A program takes and returns all parts, laid end to end along the dimension named above; each array names one. Nothing has to cross between parts.
Inputs may be any that keep to these rules, and one draw needn't show every extreme that they name: Among the live slots of one device, each owner block_cols // 8 is named at most 16 times; in every draw one owner is named exactly 16 times by the live slots of every device.
All inputs are finite; a program needn't handle non-finite values.
Results may differ from the reference program's by a relative error of at most 0.0018.
Values may be sent and summed in bfloat16 or wider, within the bound.
A program may use at most 64 MiB of HBM per device.

```python
import math
import jax
import jax.numpy as jnp
from jax import lax

BLK = 128
NB_DEV = 128
XB_DEV = 8
YB_DEV = 4
CAP = 16
ROWBLKS = 64
COLBLKS = 128
N_ROW = 8
N_COL = 2


def draw_block_cols(key, part):
    key = jax.random.fold_in(key, 11)
    key_star, key_dev = jax.random.split(key)
    star = jax.random.randint(key_star, (), 0, N_ROW)
    half = NB_DEV // 2

    def one_device(dev_key):
        key_a, key_b, key_c = jax.random.split(dev_key, 3)
        others = jax.random.permutation(key_a, (N_ROW - 1) * CAP)[:NB_DEV - CAP] // CAP
        rest = (star + 1 + others) % N_ROW
        owners = jnp.concatenate([jnp.full((CAP,), star, jnp.int32), rest.astype(jnp.int32)])
        order = jax.random.permutation(key_b, half)
        owners = jnp.concatenate([owners[:half][order], owners[half:]])
        inner = jax.random.randint(key_c, (NB_DEV,), 0, XB_DEV)
        return (owners * XB_DEV + inner).astype(jnp.int32)
    keys = jax.random.split(key_dev, N_ROW * N_COL)
    return jax.vmap(one_device)(keys).reshape(N_ROW, N_COL, NB_DEV).astype(jnp.int32)


def draw_block_counts(key, part):
    key = jax.random.fold_in(key, 12)
    key_a, key_b, key_c = jax.random.split(key, 3)
    counts = jax.random.randint(key_a, (N_ROW * N_COL,), 3 * NB_DEV // 4, NB_DEV + 1)
    fullest = jax.random.randint(key_b, (), 0, N_ROW * N_COL)
    emptiest = (fullest + 1 + jax.random.randint(key_c, (), 0, N_ROW * N_COL - 1)) % (N_ROW * N_COL)
    counts = counts.at[fullest].set(NB_DEV).at[emptiest].set(3 * NB_DEV // 4)
    return counts.reshape(N_ROW, N_COL).astype(jnp.int32)


def set_ends(entries, key, least, high):
    extent = entries.shape
    spot = [jax.random.randint(jax.random.fold_in(key, axis), (), 0, extent[axis]) for axis in range(len(extent))]
    entries = entries.at[tuple(spot)].set(least)
    longest = extent.index(max(extent))
    spot[longest] = (spot[longest] + 1) % extent[longest]
    return entries.at[tuple(spot)].set(high)


def block_levels(rng, dims, cuts, least, top_value):
    def one(position, shards_of):
        heights = jax.random.uniform(jax.random.fold_in(jax.random.fold_in(rng, 6), position), (shards_of,), jnp.float32, least / len(cuts), top_value / len(cuts))
        return jnp.repeat(jnp.exp(heights), dims[position] // shards_of).reshape((-1,) + (1,) * (len(dims) - position - 1))

    factor_of = one(*cuts[0])
    for cut in cuts[1:]:
        factor_of = factor_of * one(*cut)
    return factor_of


def gaussian(key, dims, spread, bound, cuts=(), dtype=jnp.bfloat16):
    factor_of = block_levels(key, dims, cuts, -0.22, 0.18) if cuts else 1.0
    values = jax.random.normal(key, dims, jnp.float32) * spread * factor_of
    return jnp.minimum(jnp.maximum(values, -bound), bound).astype(dtype)


def setup_inputs(seed: int = 0, part: int = 0) -> dict:
    key_of = jax.random.split(jax.random.key(seed), 16)
    part_keys = jax.random.split(jax.random.fold_in(key_of[15], part), 16)
    return {
        "blocks": gaussian(part_keys[0], (N_ROW, N_COL, NB_DEV, BLK, BLK), (NB_DEV * BLK // YB_DEV) ** -0.5, 0.09375, ((0, 8), (1, 2))),
        "block_rows": set_ends(jax.random.randint(part_keys[1], (N_ROW, N_COL, NB_DEV), 0, YB_DEV * N_COL), jax.random.fold_in(part_keys[1], 1), 0, (YB_DEV * N_COL) - 1).astype(jnp.int32),
        "block_cols": draw_block_cols(jax.random.fold_in(jax.random.fold_in(key_of[15], part), 71), part),
        "block_counts": draw_block_counts(jax.random.fold_in(jax.random.fold_in(key_of[15], part), 71), part),
        "primal": gaussian(part_keys[4], (COLBLKS, BLK), 0.5, 3.0, ((0, 16),), jnp.float32),
        "primal_bar": gaussian(part_keys[5], (COLBLKS, BLK), 0.5, 3.0, ((0, 16),), jnp.float32),
        "dual": gaussian(part_keys[6], (ROWBLKS, BLK), 1.0, 5.0, ((0, 16),), jnp.float32),
        "rhs": gaussian(part_keys[7], (ROWBLKS, BLK), 1.0, 5.0, ((0, 16),), jnp.float32),
        "cost_vec": gaussian(part_keys[8], (COLBLKS, BLK), 1.0, 5.0, ((0, 16),), jnp.float32),
        "lower": jnp.clip(-1.0 + 0.9 * jax.random.uniform(part_keys[9], (COLBLKS, BLK), jnp.float32) ** block_levels(part_keys[9], (COLBLKS, BLK), ((0, 16),), -0.2, 0.2), -1.0, -0.1),
        "upper": jnp.clip(0.1 + 0.9 * jax.random.uniform(part_keys[10], (COLBLKS, BLK), jnp.float32) ** block_levels(part_keys[10], (COLBLKS, BLK), ((0, 16),), -0.2, 0.2), 0.1, 1.0),
        "bound_kind": set_ends(jax.random.randint(part_keys[11], (COLBLKS, BLK), 0, 4), jax.random.fold_in(part_keys[11], 1), 0, 3).astype(jnp.int32),
        "row_kind": set_ends(jax.random.randint(part_keys[12], (ROWBLKS, BLK), 0, 2), jax.random.fold_in(part_keys[12], 1), 0, 1).astype(jnp.int32),
        "primal_step": jnp.clip(jnp.exp(jax.random.uniform(part_keys[13], (1,), jnp.float32, math.log(0.3), math.log(1.0))), 0.3, 1.0),
        "dual_step": jnp.clip(jnp.exp(jax.random.uniform(part_keys[14], (1,), jnp.float32, math.log(0.3), math.log(1.0))), 0.3, 1.0),
    }


def reference(blocks, block_rows, block_cols, block_counts, primal, primal_bar, dual, rhs, cost_vec, lower, upper, bound_kind, row_kind, primal_step, dual_step):
    row_blocks = YB_DEV * N_COL
    col_blocks = XB_DEV * N_ROW
    xbar = primal_bar.astype(jnp.bfloat16).reshape(N_COL, col_blocks, BLK)
    live = jnp.arange(NB_DEV)[None, None, :] < block_counts[:, :, None]
    col_ids = jnp.arange(N_COL)[:, None]

    def row_part(items):
        blk, rows, cols, alive = items
        picked = xbar[col_ids, cols].astype(jnp.float32)
        prod = jnp.einsum("cnij,cnj->cni", blk.astype(jnp.float32), picked, precision=lax.Precision.HIGHEST)
        prod = jnp.where(alive[..., None], prod, 0.0)
        onehot = (rows[..., None] == jnp.arange(row_blocks)[None, None, :]).astype(jnp.float32)
        return jnp.einsum("cnk,cni->ki", onehot, prod, precision=lax.Precision.HIGHEST)

    kx = lax.map(row_part, (blocks, block_rows, block_cols, live)).reshape(N_ROW * row_blocks, BLK)
    moved = dual + dual_step[0] * (rhs - kx)
    dual_new = jnp.where(row_kind == 1, jnp.maximum(moved, 0.0), moved)
    ybar = dual_new.astype(jnp.bfloat16).reshape(N_ROW, row_blocks, BLK)

    def col_part(total, items):
        blk, rows, cols, alive, yrows = items
        picked = yrows[rows].astype(jnp.float32)
        back = jnp.einsum("cnij,cni->cnj", blk.astype(jnp.float32), picked, precision=lax.Precision.HIGHEST)
        back = jnp.where(alive[..., None], back, 0.0)
        onehot = (cols[..., None] == jnp.arange(col_blocks)[None, None, :]).astype(jnp.float32)
        return total + jnp.einsum("cnk,cnj->ckj", onehot, back, precision=lax.Precision.HIGHEST), None

    start = jnp.zeros((N_COL, col_blocks, BLK), jnp.float32)
    kty, unused = lax.scan(col_part, start, (blocks, block_rows, block_cols, live, ybar))
    kty = kty.reshape(N_COL * col_blocks, BLK)
    moved_primal = primal - primal_step[0] * (cost_vec - kty)
    has_lower = (bound_kind == 1) | (bound_kind == 3)
    has_upper = (bound_kind == 2) | (bound_kind == 3)
    moved_primal = jnp.where(has_lower, jnp.maximum(moved_primal, lower), moved_primal)
    primal_new = jnp.where(has_upper, jnp.minimum(moved_primal, upper), moved_primal)
    return dual_new, primal_new, 2.0 * primal_new - primal
```

```python
import functools

import jax
import jax.numpy as jnp
from jax import lax
from jax.experimental import pallas as pl
from jax.experimental.pallas import tpu as pltpu
from jax.sharding import PartitionSpec as P

MESH = pl.DeviceIdType.MESH
BLOCK_CHUNKS = 4


def kernel(
    n_row,
    blocks,
    block_rows,
    block_cols,
    block_counts,
    primal,
    primal_bar,
    dual,
    rhs,
    cost_vec,
    lower,
    upper,
    bound_kind,
    row_kind,
    primal_step,
    dual_step,
    dual_out,
    primal_out,
    bar_out,
    blk,
    rows_s,
    cols_s,
    count_s,
    pstep_s,
    dstep_s,
    xall,
    dual_v,
    primal_v,
    kind_row_v,
    kind_v,
    packed,
    part,
    yall,
    kty,
    pieces,
    out_d,
    out_p,
    local_sem,
    blk_sem,
    x_send,
    x_recv,
    pair_send,
    pair_recv,
    t_send,
    t_recv,
):
    r = lax.axis_index("row")
    c = lax.axis_index("col")
    slots, size = blk.shape[0], blk.shape[1]
    xb = primal.shape[0]
    yb = dual.shape[0]
    mine = pl.ds(pl.multiple_of(r * xb, xb), xb)
    per_chunk = slots // BLOCK_CHUNKS

    def local(src, dst, i):
        copy = pltpu.make_async_copy(src, dst, local_sem.at[i])
        copy.start()
        return copy

    x_copy = local(primal_bar, xall.at[mine], 0)
    dual_copies = [
        local(dual, dual_v.at[0], 1),
        local(rhs, dual_v.at[1], 2),
        local(row_kind, kind_row_v, 3),
        local(dual_step, dstep_s, 4),
    ]
    index_copies = [
        local(block_rows.at[0], rows_s, 5),
        local(block_cols.at[0], cols_s, 6),
        local(block_counts, count_s, 7),
    ]
    blk_copies = []
    for k in range(BLOCK_CHUNKS):
        span = pl.ds(k * per_chunk, per_chunk)
        copy = pltpu.make_async_copy(blocks.at[0, 0, span], blk.at[span], blk_sem.at[k])
        copy.start()
        blk_copies.append(copy)
    primal_copies = [
        local(primal, primal_v.at[0], 8),
        local(cost_vec, primal_v.at[1], 9),
        local(lower, primal_v.at[2], 10),
        local(upper, primal_v.at[3], 11),
        local(bound_kind, kind_v, 12),
        local(primal_step, pstep_s, 13),
    ]

    def peer(k):
        return lax.rem(r + k, n_row)

    def for_peers(do):
        if n_row <= 8:
            for k in range(1, n_row):
                do(k)
        else:
            lax.fori_loop(1, n_row, lambda k, carry: (do(k), carry)[1], 0)

    barrier = pltpu.get_barrier_semaphore()
    for_peers(
        lambda k: pl.semaphore_signal(
            barrier, inc=1, device_id={"row": peer(k)}, device_id_type=MESH
        )
    )
    pl.semaphore_signal(barrier, inc=1, device_id={"col": 1 - c}, device_id_type=MESH)
    pl.semaphore_wait(barrier, n_row)

    def x_remote(k):
        return pltpu.make_async_remote_copy(
            src_ref=xall.at[mine],
            dst_ref=xall.at[mine],
            send_sem=x_send.at[k],
            recv_sem=x_recv.at[k],
            device_id={"row": peer(k)},
            device_id_type=MESH,
        )

    x_copy.wait()
    for_peers(lambda k: x_remote(k).start())

    for copy in dual_copies:
        copy.wait()
    dstep = dstep_s[0]
    packed[c, 0] = dual_v[0] + dstep * dual_v[1]
    packed[c, 1] = jnp.where(kind_row_v[...] == 1, 0.0, -jnp.inf)

    def to_pair(src, dst, i):
        return pltpu.make_async_remote_copy(
            src_ref=src,
            dst_ref=dst,
            send_sem=pair_send.at[i],
            recv_sem=pair_recv.at[i],
            device_id={"col": 1 - c},
            device_id_type=MESH,
        )

    pack_copy = to_pair(packed.at[c], packed.at[c], 0)
    pack_copy.start()

    for copy in index_copies:
        copy.wait()
    count = count_s[0, 0]
    row_iota = lax.broadcasted_iota(jnp.int32, (2 * yb, size), 0)
    col_iota = lax.broadcasted_iota(jnp.int32, (xb * n_row, size), 0)
    for copy in blk_copies:
        copy.wait()
    for_peers(lambda k: x_remote(k).wait_recv())

    def picked(n):
        live_row = jnp.where(n < count, rows_s[0, n], -1)
        return jnp.where(row_iota == live_row, xall[pl.ds(cols_s[0, n], 1), :], 0.0)

    def forward(q, acc):
        n = 4 * q
        left = jnp.concatenate(
            [
                jnp.concatenate([picked(n), picked(n + 1)], 1),
                jnp.concatenate([picked(n + 2), picked(n + 3)], 1),
            ],
            0,
        ).astype(jnp.bfloat16)
        right = jnp.concatenate(
            [
                jnp.concatenate([blk[n], blk[n + 1]], 1),
                jnp.concatenate([blk[n + 2], blk[n + 3]], 1),
            ],
            0,
        )
        return acc + lax.dot_general(
            left, right, (((1,), (1,)), ((), ())), preferred_element_type=jnp.float32
        )

    acc = jnp.zeros((4 * yb, 2 * size), jnp.float32)
    acc = lax.fori_loop(0, slots // 4, forward, acc, unroll=8)
    total = acc[: 2 * yb, :size] + acc[2 * yb :, size:]
    for h in range(2):
        part[0, h] = total[h * yb : (h + 1) * yb]
    part_copy = to_pair(part.at[0], part.at[1], 1)
    part_copy.start()
    pack_copy.wait_recv()
    part_copy.wait_recv()

    for h in range(2):
        moved = packed[h, 0] - dstep * (part[0, h] + part[1, h])
        new = jnp.maximum(moved, packed[h, 1])
        out_d[h] = new
        yall[h * yb : (h + 1) * yb, :] = new.astype(jnp.bfloat16).astype(jnp.float32)
    d_copy = local(out_d.at[c], dual_out, 14)

    def masked(n):
        live_col = jnp.where(n < count, cols_s[0, n], -1)
        return jnp.where(col_iota == live_col, yall[pl.ds(rows_s[0, n], 1), :], 0.0)

    def backward(q, acc):
        n = 2 * q
        left = jnp.concatenate([masked(n), masked(n + 1)], 1).astype(jnp.bfloat16)
        right = jnp.concatenate([blk[n], blk[n + 1]], 0)
        return acc + jnp.dot(left, right, preferred_element_type=jnp.float32)

    if n_row <= 8:
        acc = jnp.zeros((xb * n_row, size), jnp.float32)
        kty[...] = lax.fori_loop(0, slots // 2, backward, acc, unroll=8)
    else:
        kty[...] = jnp.zeros_like(kty)

        def into(q, carry):
            kty[...] = backward(q, kty[...])
            return carry

        lax.fori_loop(0, slots // 2, into, 0)

    def t_remote(k):
        theirs = pl.ds(pl.multiple_of(peer(k) * xb, xb), xb)
        return pltpu.make_async_remote_copy(
            src_ref=kty.at[theirs],
            dst_ref=pieces.at[k],
            send_sem=t_send.at[k],
            recv_sem=t_recv.at[k],
            device_id={"row": peer(k)},
            device_id_type=MESH,
        )

    for_peers(lambda k: t_remote(k).start())
    for copy in primal_copies:
        copy.wait()
    total = kty[mine, :]
    if n_row <= 8:
        for k in range(1, n_row):
            t_remote(k).wait_recv()
            total = total + pieces[k]
    else:
        for_peers(lambda k: t_remote(k).wait_recv())
        total = lax.fori_loop(1, n_row, lambda k, s: s + pieces[k], total)

    old = primal_v[0]
    kind = kind_v[...]
    moved = old - pstep_s[0] * (primal_v[1] - total)
    moved = jnp.where((kind == 1) | (kind == 3), jnp.maximum(moved, primal_v[2]), moved)
    new = jnp.where((kind == 2) | (kind == 3), jnp.minimum(moved, primal_v[3]), moved)
    out_p[0] = new
    out_p[1] = 2.0 * new - old
    p_copy = local(out_p.at[0], primal_out, 15)
    b_copy = local(out_p.at[1], bar_out, 16)

    for_peers(lambda k: x_remote(k).wait_send())
    pack_copy.wait_send()
    part_copy.wait_send()
    for_peers(lambda k: t_remote(k).wait_send())
    d_copy.wait()
    p_copy.wait()
    b_copy.wait()


def body(n_row, *args):
    blocks, block_rows, primal, dual = args[0], args[1], args[4], args[6]
    slots, size = blocks.shape[2], blocks.shape[3]
    xb, yb = primal.shape[0], dual.shape[0]
    f32, i32 = jnp.float32, jnp.int32
    dma = pltpu.SemaphoreType.DMA
    return pl.pallas_call(
        functools.partial(kernel, n_row),
        out_shape=(
            jax.ShapeDtypeStruct((yb, size), f32),
            jax.ShapeDtypeStruct((xb, size), f32),
            jax.ShapeDtypeStruct((xb, size), f32),
        ),
        in_specs=[pl.BlockSpec(memory_space=pl.ANY)] * len(args),
        out_specs=[pl.BlockSpec(memory_space=pl.ANY)] * 3,
        scratch_shapes=[
            pltpu.VMEM((slots, size, size), jnp.bfloat16),
            pltpu.SMEM((1, slots), i32),
            pltpu.SMEM((1, slots), i32),
            pltpu.SMEM((1, 1), i32),
            pltpu.SMEM((1,), f32),
            pltpu.SMEM((1,), f32),
            pltpu.VMEM((n_row * xb, size), f32),
            pltpu.VMEM((2, yb, size), f32),
            pltpu.VMEM((4, xb, size), f32),
            pltpu.VMEM((yb, size), i32),
            pltpu.VMEM((xb, size), i32),
            pltpu.VMEM((2, 2, yb, size), f32),
            pltpu.VMEM((2, 2, yb, size), f32),
            pltpu.VMEM((2 * yb, size), f32),
            pltpu.VMEM((n_row * xb, size), f32),
            pltpu.VMEM((n_row, xb, size), f32),
            pltpu.VMEM((2, yb, size), f32),
            pltpu.VMEM((2, xb, size), f32),
            dma((17,)),
            dma((BLOCK_CHUNKS,)),
            dma((n_row,)),
            dma((n_row,)),
            dma((2,)),
            dma((2,)),
            dma((n_row,)),
            dma((n_row,)),
        ],
        compiler_params=pltpu.CompilerParams(
            collective_id=0, has_side_effects=True, vmem_limit_bytes=32 * 1024 * 1024
        ),
    )(*args)


def solution(mesh):
    placed = (
        P(("groups", "row"), "col", None, None, None),
        P(("groups", "row"), "col", None),
        P(("groups", "row"), "col", None),
        P(("groups", "row"), "col"),
        P(("groups", "col", "row"), None),
        P(("groups", "col", "row"), None),
        P(("groups", "row", "col"), None),
        P(("groups", "row", "col"), None),
        P(("groups", "col", "row"), None),
        P(("groups", "col", "row"), None),
        P(("groups", "col", "row"), None),
        P(("groups", "col", "row"), None),
        P(("groups", "row", "col"), None),
        P("groups"),
        P("groups"),
    )
    return jax.shard_map(
        functools.partial(body, mesh.shape["row"]),
        mesh=mesh,
        in_specs=placed,
        out_specs=(
            P(("groups", "row", "col"), None),
            P(("groups", "col", "row"), None),
            P(("groups", "col", "row"), None),
        ),
        check_vma=False,
    )
```

```python
import functools

import jax
import jax.numpy as jnp
from jax import lax
from jax.experimental import pallas as pl
from jax.experimental.pallas import tpu as pltpu
from jax.sharding import PartitionSpec as P

MESH = pl.DeviceIdType.MESH
BLOCK_CHUNKS = 4
VMEM_BYTES = 64 * 1024 * 1024


def kernel(
    n_row,
    blocks,
    block_rows,
    block_cols,
    block_counts,
    primal,
    primal_bar,
    dual,
    rhs,
    cost_vec,
    lower,
    upper,
    bound_kind,
    row_kind,
    primal_step,
    dual_step,
    dual_out,
    primal_out,
    bar_out,
    blk,
    rows_s,
    cols_s,
    count_s,
    pstep_s,
    dstep_s,
    xall,
    dual_v,
    primal_v,
    kind_row_v,
    kind_v,
    packed,
    part,
    yall,
    kty,
    pieces,
    out_d,
    out_p,
    local_sem,
    blk_sem,
    x_send,
    x_recv,
    pair_send,
    pair_recv,
    t_send,
    t_recv,
):
    r = lax.axis_index("row")
    c = lax.axis_index("col")
    slots, size = blk.shape[0], blk.shape[1]
    xb = primal.shape[0]
    yb = dual.shape[0]
    mine = pl.ds(pl.multiple_of(r * xb, xb), xb)
    per_chunk = slots // BLOCK_CHUNKS

    def local(src, dst, i):
        copy = pltpu.make_async_copy(src, dst, local_sem.at[i])
        copy.start()
        return copy

    x_copy = local(primal_bar, xall.at[mine], 0)
    dual_copies = [
        local(dual, dual_v.at[0], 1),
        local(rhs, dual_v.at[1], 2),
        local(row_kind, kind_row_v, 3),
        local(dual_step, dstep_s, 4),
    ]
    index_copies = [
        local(block_rows.at[0], rows_s, 5),
        local(block_cols.at[0], cols_s, 6),
        local(block_counts, count_s, 7),
    ]
    blk_copies = []
    for k in range(BLOCK_CHUNKS):
        span = pl.ds(k * per_chunk, per_chunk)
        copy = pltpu.make_async_copy(blocks.at[0, 0, span], blk.at[span], blk_sem.at[k])
        copy.start()
        blk_copies.append(copy)
    primal_copies = [
        local(primal, primal_v.at[0], 8),
        local(cost_vec, primal_v.at[1], 9),
        local(lower, primal_v.at[2], 10),
        local(upper, primal_v.at[3], 11),
        local(bound_kind, kind_v, 12),
        local(primal_step, pstep_s, 13),
    ]

    def peer(k):
        return lax.rem(r + k, n_row)

    def for_peers(do):
        if n_row <= 8:
            for k in range(1, n_row):
                do(k)
        else:
            lax.fori_loop(1, n_row, lambda k, carry: (do(k), carry)[1], 0)

    barrier = pltpu.get_barrier_semaphore()
    for_peers(
        lambda k: pl.semaphore_signal(
            barrier, inc=1, device_id={"row": peer(k)}, device_id_type=MESH
        )
    )
    pl.semaphore_signal(barrier, inc=1, device_id={"col": 1 - c}, device_id_type=MESH)
    pl.semaphore_wait(barrier, n_row)

    def x_remote(k):
        return pltpu.make_async_remote_copy(
            src_ref=xall.at[mine],
            dst_ref=xall.at[mine],
            send_sem=x_send.at[k],
            recv_sem=x_recv.at[k],
            device_id={"row": peer(k)},
            device_id_type=MESH,
        )

    x_copy.wait()
    for_peers(lambda k: x_remote(k).start())

    for copy in dual_copies:
        copy.wait()
    dstep = dstep_s[0]
    packed[c, 0] = dual_v[0] + dstep * dual_v[1]
    packed[c, 1] = jnp.where(kind_row_v[...] == 1, 0.0, -jnp.inf)

    def to_pair(src, dst, i):
        return pltpu.make_async_remote_copy(
            src_ref=src,
            dst_ref=dst,
            send_sem=pair_send.at[i],
            recv_sem=pair_recv.at[i],
            device_id={"col": 1 - c},
            device_id_type=MESH,
        )

    pack_copy = to_pair(packed.at[c], packed.at[c], 0)
    pack_copy.start()

    for copy in index_copies:
        copy.wait()
    count = count_s[0, 0]
    row_iota = lax.broadcasted_iota(jnp.int32, (2 * yb, size), 0)
    col_iota = lax.broadcasted_iota(jnp.int32, (xb * n_row, size), 0)
    for copy in blk_copies:
        copy.wait()
    for_peers(lambda k: x_remote(k).wait_recv())

    def picked(n):
        live_row = jnp.where(n < count, rows_s[0, n], -1)
        return jnp.where(row_iota == live_row, xall[pl.ds(cols_s[0, n], 1), :], 0.0)

    def forward(q, acc):
        n = 4 * q
        left = jnp.concatenate(
            [
                jnp.concatenate([picked(n), picked(n + 1)], 1),
                jnp.concatenate([picked(n + 2), picked(n + 3)], 1),
            ],
            0,
        ).astype(jnp.bfloat16)
        right = jnp.concatenate(
            [
                jnp.concatenate([blk[n], blk[n + 1]], 1),
                jnp.concatenate([blk[n + 2], blk[n + 3]], 1),
            ],
            0,
        )
        return acc + lax.dot_general(
            left, right, (((1,), (1,)), ((), ())), preferred_element_type=jnp.float32
        )

    acc = jnp.zeros((4 * yb, 2 * size), jnp.float32)
    acc = lax.fori_loop(0, slots // 4, forward, acc, unroll=8)
    total = acc[: 2 * yb, :size] + acc[2 * yb :, size:]
    for h in range(2):
        part[0, h] = total[h * yb : (h + 1) * yb]
    part_copy = to_pair(part.at[0], part.at[1], 1)
    part_copy.start()
    pack_copy.wait_recv()
    part_copy.wait_recv()

    for h in range(2):
        moved = packed[h, 0] - dstep * (part[0, h] + part[1, h])
        new = jnp.maximum(moved, packed[h, 1])
        out_d[h] = new
        yall[h * yb : (h + 1) * yb, :] = new.astype(jnp.bfloat16).astype(jnp.float32)
    d_copy = local(out_d.at[c], dual_out, 14)

    def masked(n):
        live_col = jnp.where(n < count, cols_s[0, n], -1)
        return jnp.where(col_iota == live_col, yall[pl.ds(rows_s[0, n], 1), :], 0.0)

    def backward(q, acc):
        n = 2 * q
        left = jnp.concatenate([masked(n), masked(n + 1)], 1).astype(jnp.bfloat16)
        right = jnp.concatenate([blk[n], blk[n + 1]], 0)
        return acc + jnp.dot(left, right, preferred_element_type=jnp.float32)

    if n_row <= 8:
        acc = jnp.zeros((xb * n_row, size), jnp.float32)
        kty[...] = lax.fori_loop(0, slots // 2, backward, acc, unroll=8)
    else:
        kty[...] = jnp.zeros_like(kty)

        def into(q, carry):
            kty[...] = backward(q, kty[...])
            return carry

        lax.fori_loop(0, slots // 2, into, 0)

    def t_remote(k):
        theirs = pl.ds(pl.multiple_of(peer(k) * xb, xb), xb)
        return pltpu.make_async_remote_copy(
            src_ref=kty.at[theirs],
            dst_ref=pieces.at[k],
            send_sem=t_send.at[k],
            recv_sem=t_recv.at[k],
            device_id={"row": peer(k)},
            device_id_type=MESH,
        )

    for_peers(lambda k: t_remote(k).start())
    for copy in primal_copies:
        copy.wait()
    total = kty[mine, :]
    if n_row <= 8:
        for k in range(1, n_row):
            t_remote(k).wait_recv()
            total = total + pieces[k]
    else:
        for_peers(lambda k: t_remote(k).wait_recv())
        total = lax.fori_loop(1, n_row, lambda k, s: s + pieces[k], total)

    old = primal_v[0]
    kind = kind_v[...]
    moved = old - pstep_s[0] * (primal_v[1] - total)
    moved = jnp.where((kind == 1) | (kind == 3), jnp.maximum(moved, primal_v[2]), moved)
    new = jnp.where((kind == 2) | (kind == 3), jnp.minimum(moved, primal_v[3]), moved)
    out_p[0] = new
    out_p[1] = 2.0 * new - old
    p_copy = local(out_p.at[0], primal_out, 15)
    b_copy = local(out_p.at[1], bar_out, 16)

    for_peers(lambda k: x_remote(k).wait_send())
    pack_copy.wait_send()
    part_copy.wait_send()
    for_peers(lambda k: t_remote(k).wait_send())
    d_copy.wait()
    p_copy.wait()
    b_copy.wait()


def hand_out_kernel(dual_v, primal_v, bar_v, dual_out, primal_out, bar_out, sem):
    copies = [
        pltpu.make_async_copy(src, dst, sem.at[i])
        for i, (src, dst) in enumerate(
            ((dual_v, dual_out), (primal_v, primal_out), (bar_v, bar_out))
        )
    ]
    for copy in copies:
        copy.start()
    for copy in copies:
        copy.wait()


def hand_out(*results):
    return pl.pallas_call(
        hand_out_kernel,
        out_shape=tuple(jax.ShapeDtypeStruct(a.shape, a.dtype) for a in results),
        in_specs=[pl.BlockSpec(memory_space=pltpu.HBM)] * 3,
        out_specs=[pl.BlockSpec(memory_space=pltpu.HBM)] * 3,
        scratch_shapes=[pltpu.SemaphoreType.DMA((3,))],
        compiler_params=pltpu.CompilerParams(vmem_limit_bytes=VMEM_BYTES),
    )(*results)


def body(n_row, *args):
    blocks, block_rows, primal, dual = args[0], args[1], args[4], args[6]
    slots, size = blocks.shape[2], blocks.shape[3]
    xb, yb = primal.shape[0], dual.shape[0]
    f32, i32 = jnp.float32, jnp.int32
    dma = pltpu.SemaphoreType.DMA
    results = pl.pallas_call(
        functools.partial(kernel, n_row),
        out_shape=(
            jax.ShapeDtypeStruct((yb, size), f32),
            jax.ShapeDtypeStruct((xb, size), f32),
            jax.ShapeDtypeStruct((xb, size), f32),
        ),
        in_specs=[pl.BlockSpec(memory_space=pltpu.HBM)] * len(args),
        out_specs=[pl.BlockSpec(memory_space=pltpu.HBM)] * 3,
        scratch_shapes=[
            pltpu.VMEM((slots, size, size), jnp.bfloat16),
            pltpu.SMEM((1, slots), i32),
            pltpu.SMEM((1, slots), i32),
            pltpu.SMEM((1, 1), i32),
            pltpu.SMEM((1,), f32),
            pltpu.SMEM((1,), f32),
            pltpu.VMEM((n_row * xb, size), f32),
            pltpu.VMEM((2, yb, size), f32),
            pltpu.VMEM((4, xb, size), f32),
            pltpu.VMEM((yb, size), i32),
            pltpu.VMEM((xb, size), i32),
            pltpu.VMEM((2, 2, yb, size), f32),
            pltpu.VMEM((2, 2, yb, size), f32),
            pltpu.VMEM((2 * yb, size), f32),
            pltpu.VMEM((n_row * xb, size), f32),
            pltpu.VMEM((n_row, xb, size), f32),
            pltpu.VMEM((2, yb, size), f32),
            pltpu.VMEM((2, xb, size), f32),
            dma((17,)),
            dma((BLOCK_CHUNKS,)),
            dma((n_row,)),
            dma((n_row,)),
            dma((2,)),
            dma((2,)),
            dma((n_row,)),
            dma((n_row,)),
        ],
        compiler_params=pltpu.CompilerParams(
            collective_id=0, has_side_effects=True, vmem_limit_bytes=VMEM_BYTES
        ),
    )(*args)
    return hand_out(*results)


def solution(mesh):
    placed = (
        P(("groups", "row"), "col", None, None, None),
        P(("groups", "row"), "col", None),
        P(("groups", "row"), "col", None),
        P(("groups", "row"), "col"),
        P(("groups", "col", "row"), None),
        P(("groups", "col", "row"), None),
        P(("groups", "row", "col"), None),
        P(("groups", "row", "col"), None),
        P(("groups", "col", "row"), None),
        P(("groups", "col", "row"), None),
        P(("groups", "col", "row"), None),
        P(("groups", "col", "row"), None),
        P(("groups", "row", "col"), None),
        P("groups"),
        P("groups"),
    )
    return jax.shard_map(
        functools.partial(body, mesh.shape["row"]),
        mesh=mesh,
        in_specs=placed,
        out_specs=(
            P(("groups", "row", "col"), None),
            P(("groups", "col", "row"), None),
            P(("groups", "col", "row"), None),
        ),
        check_vma=False,
    )
```

```python
import functools

import jax
import jax.numpy as jnp
from jax import lax
from jax.experimental import pallas as pl
from jax.experimental.pallas import tpu as pltpu
from jax.sharding import PartitionSpec as P

MESH = pl.DeviceIdType.MESH
BLOCK_CHUNKS = 4
VMEM_BYTES = 32 * 1024 * 1024


def kernel(
    n_row,
    blocks,
    block_rows,
    block_cols,
    block_counts,
    primal,
    primal_bar,
    dual,
    rhs,
    cost_vec,
    lower,
    upper,
    bound_kind,
    row_kind,
    primal_step,
    dual_step,
    dual_out,
    primal_out,
    bar_out,
    blk,
    rows_s,
    cols_s,
    count_s,
    pstep_s,
    dstep_s,
    xall,
    dual_v,
    primal_v,
    kind_row_v,
    kind_v,
    packed,
    part,
    yall,
    kty,
    pieces,
    local_sem,
    blk_sem,
    x_send,
    x_recv,
    pair_send,
    pair_recv,
    t_send,
    t_recv,
):
    r = lax.axis_index("row")
    c = lax.axis_index("col")
    slots, size = blk.shape[0], blk.shape[1]
    xb = primal.shape[0]
    yb = dual.shape[0]
    mine = pl.ds(pl.multiple_of(r * xb, xb), xb)
    per_chunk = slots // BLOCK_CHUNKS

    def local(src, dst, i):
        copy = pltpu.make_async_copy(src, dst, local_sem.at[i])
        copy.start()
        return copy

    x_copy = local(primal_bar, xall.at[mine], 0)

    def peer(k):
        if n_row > 8:
            return lax.rem(r + k, n_row)
        other = r
        for b in (1, 2, 4):
            if k & b:
                other = other + b * (1 - 2 * lax.rem(r // b, 2))
        return other

    def for_peers(do):
        if n_row <= 8:
            for k in range(n_row - 1, 0, -1):
                do(k)
        else:
            lax.fori_loop(1, n_row, lambda k, carry: (do(k), carry)[1], 0)

    barrier = pltpu.get_barrier_semaphore()
    for_peers(
        lambda k: pl.semaphore_signal(
            barrier, inc=1, device_id={"row": peer(k)}, device_id_type=MESH
        )
    )
    pl.semaphore_signal(barrier, inc=1, device_id={"col": 1 - c}, device_id_type=MESH)

    dual_copies = [
        local(dual, dual_v.at[0], 1),
        local(rhs, dual_v.at[1], 2),
        local(row_kind, kind_row_v, 3),
        local(dual_step, dstep_s, 4),
    ]
    index_copies = [
        local(block_rows.at[0], rows_s, 5),
        local(block_cols.at[0], cols_s, 6),
        local(block_counts, count_s, 7),
    ]
    blk_copies = []
    for k in range(BLOCK_CHUNKS):
        span = pl.ds(k * per_chunk, per_chunk)
        copy = pltpu.make_async_copy(blocks.at[0, 0, span], blk.at[span], blk_sem.at[k])
        copy.start()
        blk_copies.append(copy)
    primal_copies = [
        local(primal, primal_v.at[0], 8),
        local(cost_vec, primal_v.at[1], 9),
        local(lower, primal_v.at[2], 10),
        local(upper, primal_v.at[3], 11),
        local(bound_kind, kind_v, 12),
        local(primal_step, pstep_s, 13),
    ]

    pl.semaphore_wait(barrier, n_row)

    def x_remote(k):
        return pltpu.make_async_remote_copy(
            src_ref=xall.at[mine],
            dst_ref=xall.at[mine],
            send_sem=x_send.at[k],
            recv_sem=x_recv.at[k],
            device_id={"row": peer(k)},
            device_id_type=MESH,
        )

    x_copy.wait()
    for_peers(lambda k: x_remote(k).start())

    for copy in dual_copies:
        copy.wait()
    dstep = dstep_s[0]
    packed[c, 0] = dual_v[0] + dstep * dual_v[1]
    packed[c, 1] = jnp.where(kind_row_v[...] == 1, 0.0, -jnp.inf)

    def to_pair(src, dst, i):
        return pltpu.make_async_remote_copy(
            src_ref=src,
            dst_ref=dst,
            send_sem=pair_send.at[i],
            recv_sem=pair_recv.at[i],
            device_id={"col": 1 - c},
            device_id_type=MESH,
        )

    pack_copy = to_pair(packed.at[c], packed.at[c], 0)
    pack_copy.start()

    for copy in index_copies:
        copy.wait()
    count = count_s[0, 0]
    row_iota = lax.broadcasted_iota(jnp.int32, (2 * yb, size), 0)
    col_iota = lax.broadcasted_iota(jnp.int32, (xb * n_row, size), 0)
    for copy in blk_copies:
        copy.wait()
    for_peers(lambda k: x_remote(k).wait_recv())

    def picked(n):
        live_row = jnp.where(n < count, rows_s[0, n], -1)
        return jnp.where(row_iota == live_row, xall[pl.ds(cols_s[0, n], 1), :], 0.0)

    def forward(q, acc):
        n = 4 * q
        left = jnp.concatenate(
            [
                jnp.concatenate([picked(n), picked(n + 1)], 1),
                jnp.concatenate([picked(n + 2), picked(n + 3)], 1),
            ],
            0,
        ).astype(jnp.bfloat16)
        right = jnp.concatenate(
            [
                jnp.concatenate([blk[n], blk[n + 1]], 1),
                jnp.concatenate([blk[n + 2], blk[n + 3]], 1),
            ],
            0,
        )
        return acc + lax.dot_general(
            left, right, (((1,), (1,)), ((), ())), preferred_element_type=jnp.float32
        )

    acc = jnp.zeros((4 * yb, 2 * size), jnp.float32)
    acc = lax.fori_loop(0, slots // 4, forward, acc, unroll=16)
    total = acc[: 2 * yb, :size] + acc[2 * yb :, size:]
    for h in range(2):
        part[0, h] = total[h * yb : (h + 1) * yb]
    part_copy = to_pair(part.at[0], part.at[1], 1)
    part_copy.start()
    pack_copy.wait_recv()
    part_copy.wait_recv()

    news = []
    for h in range(2):
        moved = packed[h, 0] - dstep * (part[0, h] + part[1, h])
        new = jnp.maximum(moved, packed[h, 1])
        news.append(new)
        yall[h * yb : (h + 1) * yb, :] = new.astype(jnp.bfloat16).astype(jnp.float32)
    dual_out[...] = jnp.where(c == 0, news[0], news[1])

    def masked(n):
        live_col = jnp.where(n < count, cols_s[0, n], -1)
        return jnp.where(col_iota == live_col, yall[pl.ds(rows_s[0, n], 1), :], 0.0)

    def backward(q, acc):
        n = 2 * q
        left = jnp.concatenate([masked(n), masked(n + 1)], 1).astype(jnp.bfloat16)
        right = jnp.concatenate([blk[n], blk[n + 1]], 0)
        return acc + jnp.dot(left, right, preferred_element_type=jnp.float32)

    if n_row <= 8:
        acc = jnp.zeros((xb * n_row, size), jnp.float32)
        kty[...] = lax.fori_loop(0, slots // 2, backward, acc, unroll=32)
    else:
        kty[...] = jnp.zeros_like(kty)

        def into(q, carry):
            kty[...] = backward(q, kty[...])
            return carry

        lax.fori_loop(0, slots // 2, into, 0)

    def t_remote(k):
        theirs = pl.ds(pl.multiple_of(peer(k) * xb, xb), xb)
        return pltpu.make_async_remote_copy(
            src_ref=kty.at[theirs],
            dst_ref=pieces.at[k],
            send_sem=t_send.at[k],
            recv_sem=t_recv.at[k],
            device_id={"row": peer(k)},
            device_id_type=MESH,
        )

    for_peers(lambda k: t_remote(k).start())
    for copy in primal_copies:
        copy.wait()
    total = kty[mine, :]
    if n_row <= 8:
        for k in range(1, n_row):
            t_remote(k).wait_recv()
            total = total + pieces[k]
    else:
        for_peers(lambda k: t_remote(k).wait_recv())
        total = lax.fori_loop(1, n_row, lambda k, s: s + pieces[k], total)

    old = primal_v[0]
    kind = kind_v[...]
    moved = old - pstep_s[0] * (primal_v[1] - total)
    moved = jnp.where((kind == 1) | (kind == 3), jnp.maximum(moved, primal_v[2]), moved)
    new = jnp.where((kind == 2) | (kind == 3), jnp.minimum(moved, primal_v[3]), moved)
    primal_out[...] = new
    bar_out[...] = 2.0 * new - old

    for_peers(lambda k: x_remote(k).wait_send())
    pack_copy.wait_send()
    part_copy.wait_send()
    for_peers(lambda k: t_remote(k).wait_send())


def hand_out_kernel(dual_v, primal_v, bar_v, dual_out, primal_out, bar_out, sem):
    copies = [
        pltpu.make_async_copy(src, dst, sem.at[i])
        for i, (src, dst) in enumerate(
            ((dual_v, dual_out), (primal_v, primal_out), (bar_v, bar_out))
        )
    ]
    for copy in copies:
        copy.start()
    for copy in copies:
        copy.wait()


def hand_out(*results):
    return pl.pallas_call(
        hand_out_kernel,
        out_shape=tuple(jax.ShapeDtypeStruct(a.shape, a.dtype) for a in results),
        in_specs=[pl.BlockSpec(memory_space=pltpu.VMEM)] * 3,
        out_specs=[pl.BlockSpec(memory_space=pltpu.HBM)] * 3,
        scratch_shapes=[pltpu.SemaphoreType.DMA((3,))],
        compiler_params=pltpu.CompilerParams(vmem_limit_bytes=VMEM_BYTES),
    )(*results)


def body(n_row, *args):
    blocks, block_rows, primal, dual = args[0], args[1], args[4], args[6]
    slots, size = blocks.shape[2], blocks.shape[3]
    xb, yb = primal.shape[0], dual.shape[0]
    f32, i32 = jnp.float32, jnp.int32
    dma = pltpu.SemaphoreType.DMA
    results = pl.pallas_call(
        functools.partial(kernel, n_row),
        out_shape=(
            pltpu.VMEM((yb, size), f32),
            pltpu.VMEM((xb, size), f32),
            pltpu.VMEM((xb, size), f32),
        ),
        in_specs=[pl.BlockSpec(memory_space=pltpu.HBM)] * len(args),
        out_specs=[pl.BlockSpec(memory_space=pltpu.VMEM)] * 3,
        scratch_shapes=[
            pltpu.VMEM((slots, size, size), jnp.bfloat16),
            pltpu.SMEM((1, slots), i32),
            pltpu.SMEM((1, slots), i32),
            pltpu.SMEM((1, 1), i32),
            pltpu.SMEM((1,), f32),
            pltpu.SMEM((1,), f32),
            pltpu.VMEM((n_row * xb, size), f32),
            pltpu.VMEM((2, yb, size), f32),
            pltpu.VMEM((4, xb, size), f32),
            pltpu.VMEM((yb, size), i32),
            pltpu.VMEM((xb, size), i32),
            pltpu.VMEM((2, 2, yb, size), f32),
            pltpu.VMEM((2, 2, yb, size), f32),
            pltpu.VMEM((2 * yb, size), f32),
            pltpu.VMEM((n_row * xb, size), f32),
            pltpu.VMEM((n_row, xb, size), f32),
            dma((14,)),
            dma((BLOCK_CHUNKS,)),
            dma((n_row,)),
            dma((n_row,)),
            dma((2,)),
            dma((2,)),
            dma((n_row,)),
            dma((n_row,)),
        ],
        compiler_params=pltpu.CompilerParams(
            collective_id=0, has_side_effects=True, vmem_limit_bytes=VMEM_BYTES
        ),
    )(*[a if a.size == 1 else pltpu.with_memory_space_constraint(a, pltpu.HBM) for a in args])
    return hand_out(*results)


def solution(mesh):
    placed = (
        P(("groups", "row"), "col", None, None, None),
        P(("groups", "row"), "col", None),
        P(("groups", "row"), "col", None),
        P(("groups", "row"), "col"),
        P(("groups", "col", "row"), None),
        P(("groups", "col", "row"), None),
        P(("groups", "row", "col"), None),
        P(("groups", "row", "col"), None),
        P(("groups", "col", "row"), None),
        P(("groups", "col", "row"), None),
        P(("groups", "col", "row"), None),
        P(("groups", "col", "row"), None),
        P(("groups", "row", "col"), None),
        P("groups"),
        P("groups"),
    )
    return jax.shard_map(
        functools.partial(body, mesh.shape["row"]),
        mesh=mesh,
        in_specs=placed,
        out_specs=(
            P(("groups", "row", "col"), None),
            P(("groups", "col", "row"), None),
            P(("groups", "col", "row"), None),
        ),
        check_vma=False,
    )
```

```python
import functools

import jax
import jax.numpy as jnp
from jax import lax
from jax.experimental import pallas as pl
from jax.experimental.pallas import tpu as pltpu
from jax.sharding import PartitionSpec as P

MESH = pl.DeviceIdType.MESH
BLOCK_CHUNKS = 4
KX_SLOTS = 16
KTY_SLOTS = 16
VMEM_BYTES = 32 * 1024 * 1024


def kernel(
    n_row,
    blocks,
    block_rows,
    block_cols,
    block_counts,
    primal,
    primal_bar,
    dual,
    rhs,
    cost_vec,
    lower,
    upper,
    bound_kind,
    row_kind,
    primal_step,
    dual_step,
    dual_out,
    primal_out,
    bar_out,
    blk,
    turned,
    rows_s,
    cols_s,
    count_s,
    pstep_s,
    dstep_s,
    xall,
    dual_v,
    primal_v,
    kind_row_v,
    kind_v,
    packed,
    part,
    yall,
    kty,
    pieces,
    local_sem,
    blk_sem,
    x_send,
    x_recv,
    pair_send,
    pair_recv,
    t_send,
    t_recv,
):
    r = lax.axis_index("row")
    c = lax.axis_index("col")
    slots, size = blk.shape[0], blk.shape[1]
    xb = primal.shape[0]
    yb = dual.shape[0]
    mine = pl.ds(pl.multiple_of(r * xb, xb), xb)
    per_chunk = slots // BLOCK_CHUNKS

    def local(src, dst, i):
        copy = pltpu.make_async_copy(src, dst, local_sem.at[i])
        copy.start()
        return copy

    x_copy = local(primal_bar, xall.at[mine], 0)

    def peer(k):
        if n_row > 8:
            return lax.rem(r + k, n_row)
        other = r
        for b in (1, 2, 4):
            if k & b:
                other = other + b * (1 - 2 * lax.rem(r // b, 2))
        return other

    def for_peers(do):
        if n_row <= 8:
            for k in range(n_row - 1, 0, -1):
                do(k)
        else:
            lax.fori_loop(1, n_row, lambda k, carry: (do(k), carry)[1], 0)

    barrier = pltpu.get_barrier_semaphore()
    for_peers(
        lambda k: pl.semaphore_signal(
            barrier, inc=1, device_id={"row": peer(k)}, device_id_type=MESH
        )
    )
    pl.semaphore_signal(barrier, inc=1, device_id={"col": 1 - c}, device_id_type=MESH)

    dual_copies = [
        local(dual, dual_v.at[0], 1),
        local(rhs, dual_v.at[1], 2),
        local(row_kind, kind_row_v, 3),
        local(dual_step, dstep_s, 4),
    ]
    index_copies = [
        local(block_rows.at[0], rows_s, 5),
        local(block_cols.at[0], cols_s, 6),
        local(block_counts, count_s, 7),
    ]
    blk_copies = []
    for k in range(BLOCK_CHUNKS):
        span = pl.ds(k * per_chunk, per_chunk)
        copy = pltpu.make_async_copy(blocks.at[0, 0, span], blk.at[span], blk_sem.at[k])
        copy.start()
        blk_copies.append(copy)
    primal_copies = [
        local(primal, primal_v.at[0], 8),
        local(cost_vec, primal_v.at[1], 9),
        local(lower, primal_v.at[2], 10),
        local(upper, primal_v.at[3], 11),
        local(bound_kind, kind_v, 12),
        local(primal_step, pstep_s, 13),
    ]

    pl.semaphore_wait(barrier, n_row)

    def x_remote(k):
        return pltpu.make_async_remote_copy(
            src_ref=xall.at[mine],
            dst_ref=xall.at[mine],
            send_sem=x_send.at[k],
            recv_sem=x_recv.at[k],
            device_id={"row": peer(k)},
            device_id_type=MESH,
        )

    x_copy.wait()
    for_peers(lambda k: x_remote(k).start())

    for copy in dual_copies:
        copy.wait()
    dstep = dstep_s[0]
    packed[c, 0] = dual_v[0] + dstep * dual_v[1]
    packed[c, 1] = jnp.where(kind_row_v[...] == 1, 0.0, -jnp.inf)

    def to_pair(src, dst, i):
        return pltpu.make_async_remote_copy(
            src_ref=src,
            dst_ref=dst,
            send_sem=pair_send.at[i],
            recv_sem=pair_recv.at[i],
            device_id={"col": 1 - c},
            device_id_type=MESH,
        )

    pack_copy = to_pair(packed.at[c], packed.at[c], 0)
    pack_copy.start()

    for copy in index_copies:
        copy.wait()
    count = count_s[0, 0]
    row_iota = lax.broadcasted_iota(jnp.int32, (2 * yb, size), 0)
    col_iota = lax.broadcasted_iota(jnp.int32, (xb * n_row, size), 0)
    def turn(n, carry):
        turned[n] = blk[n].T
        return carry

    for k in range(BLOCK_CHUNKS):
        blk_copies[k].wait()
        lax.fori_loop(k * per_chunk, (k + 1) * per_chunk, turn, 0, unroll=8)
    for_peers(lambda k: x_remote(k).wait_recv())

    def picked(n):
        live_row = jnp.where(n < count, rows_s[0, n], -1)
        return jnp.where(row_iota == live_row, xall[pl.ds(cols_s[0, n], 1), :], 0.0)

    def forward(q, acc):
        n = KX_SLOTS * q
        left = jnp.concatenate([picked(n + i).astype(jnp.bfloat16) for i in range(KX_SLOTS)], 1)
        right = turned[pl.ds(n, KX_SLOTS)].reshape(KX_SLOTS * size, size)
        return acc + jnp.dot(left, right, preferred_element_type=jnp.float32)

    acc = jnp.zeros((2 * yb, size), jnp.float32)
    total = lax.fori_loop(0, slots // KX_SLOTS, forward, acc, unroll=4)
    for h in range(2):
        part[0, h] = total[h * yb : (h + 1) * yb]
    part_copy = to_pair(part.at[0], part.at[1], 1)
    part_copy.start()
    pack_copy.wait_recv()
    part_copy.wait_recv()

    news = []
    for h in range(2):
        moved = packed[h, 0] - dstep * (part[0, h] + part[1, h])
        new = jnp.maximum(moved, packed[h, 1])
        news.append(new)
        yall[h * yb : (h + 1) * yb, :] = new.astype(jnp.bfloat16).astype(jnp.float32)
    dual_out[...] = jnp.where(c == 0, news[0], news[1])

    def masked(n):
        live_col = jnp.where(n < count, cols_s[0, n], -1)
        return jnp.where(col_iota == live_col, yall[pl.ds(rows_s[0, n], 1), :], 0.0)

    def backward(q, acc):
        n = KTY_SLOTS * q
        left = jnp.concatenate([masked(n + i).astype(jnp.bfloat16) for i in range(KTY_SLOTS)], 1)
        right = blk[pl.ds(n, KTY_SLOTS)].reshape(KTY_SLOTS * size, size)
        return acc + jnp.dot(left, right, preferred_element_type=jnp.float32)

    if n_row <= 8:
        acc = jnp.zeros((xb * n_row, size), jnp.float32)
        kty[...] = lax.fori_loop(0, slots // KTY_SLOTS, backward, acc, unroll=4)
    else:
        kty[...] = jnp.zeros_like(kty)

        def into(q, carry):
            kty[...] = backward(q, kty[...])
            return carry

        lax.fori_loop(0, slots // KTY_SLOTS, into, 0)

    def t_remote(k):
        theirs = pl.ds(pl.multiple_of(peer(k) * xb, xb), xb)
        return pltpu.make_async_remote_copy(
            src_ref=kty.at[theirs],
            dst_ref=pieces.at[k],
            send_sem=t_send.at[k],
            recv_sem=t_recv.at[k],
            device_id={"row": peer(k)},
            device_id_type=MESH,
        )

    for_peers(lambda k: t_remote(k).start())
    for copy in primal_copies:
        copy.wait()
    total = kty[mine, :]
    if n_row <= 8:
        for k in range(1, n_row):
            t_remote(k).wait_recv()
            total = total + pieces[k]
    else:
        for_peers(lambda k: t_remote(k).wait_recv())
        total = lax.fori_loop(1, n_row, lambda k, s: s + pieces[k], total)

    old = primal_v[0]
    kind = kind_v[...]
    moved = old - pstep_s[0] * (primal_v[1] - total)
    moved = jnp.where((kind == 1) | (kind == 3), jnp.maximum(moved, primal_v[2]), moved)
    new = jnp.where((kind == 2) | (kind == 3), jnp.minimum(moved, primal_v[3]), moved)
    primal_out[...] = new
    bar_out[...] = 2.0 * new - old

    for_peers(lambda k: x_remote(k).wait_send())
    pack_copy.wait_send()
    part_copy.wait_send()
    for_peers(lambda k: t_remote(k).wait_send())


def hand_out_kernel(dual_v, primal_v, bar_v, dual_out, primal_out, bar_out, sem):
    copies = [
        pltpu.make_async_copy(src, dst, sem.at[i])
        for i, (src, dst) in enumerate(
            ((dual_v, dual_out), (primal_v, primal_out), (bar_v, bar_out))
        )
    ]
    for copy in copies:
        copy.start()
    for copy in copies:
        copy.wait()


def hand_out(*results):
    return pl.pallas_call(
        hand_out_kernel,
        out_shape=tuple(jax.ShapeDtypeStruct(a.shape, a.dtype) for a in results),
        in_specs=[pl.BlockSpec(memory_space=pltpu.VMEM)] * 3,
        out_specs=[pl.BlockSpec(memory_space=pltpu.HBM)] * 3,
        scratch_shapes=[pltpu.SemaphoreType.DMA((3,))],
        compiler_params=pltpu.CompilerParams(vmem_limit_bytes=VMEM_BYTES),
    )(*results)


def body(n_row, *args):
    blocks, block_rows, primal, dual = args[0], args[1], args[4], args[6]
    slots, size = blocks.shape[2], blocks.shape[3]
    xb, yb = primal.shape[0], dual.shape[0]
    f32, i32 = jnp.float32, jnp.int32
    dma = pltpu.SemaphoreType.DMA
    results = pl.pallas_call(
        functools.partial(kernel, n_row),
        out_shape=(
            pltpu.VMEM((yb, size), f32),
            pltpu.VMEM((xb, size), f32),
            pltpu.VMEM((xb, size), f32),
        ),
        in_specs=[pl.BlockSpec(memory_space=pltpu.HBM)] * len(args),
        out_specs=[pl.BlockSpec(memory_space=pltpu.VMEM)] * 3,
        scratch_shapes=[
            pltpu.VMEM((slots, size, size), jnp.bfloat16),
            pltpu.VMEM((slots, size, size), jnp.bfloat16),
            pltpu.SMEM((1, slots), i32),
            pltpu.SMEM((1, slots), i32),
            pltpu.SMEM((1, 1), i32),
            pltpu.SMEM((1,), f32),
            pltpu.SMEM((1,), f32),
            pltpu.VMEM((n_row * xb, size), f32),
            pltpu.VMEM((2, yb, size), f32),
            pltpu.VMEM((4, xb, size), f32),
            pltpu.VMEM((yb, size), i32),
            pltpu.VMEM((xb, size), i32),
            pltpu.VMEM((2, 2, yb, size), f32),
            pltpu.VMEM((2, 2, yb, size), f32),
            pltpu.VMEM((2 * yb, size), f32),
            pltpu.VMEM((n_row * xb, size), f32),
            pltpu.VMEM((n_row, xb, size), f32),
            dma((14,)),
            dma((BLOCK_CHUNKS,)),
            dma((n_row,)),
            dma((n_row,)),
            dma((2,)),
            dma((2,)),
            dma((n_row,)),
            dma((n_row,)),
        ],
        compiler_params=pltpu.CompilerParams(
            collective_id=0, has_side_effects=True, vmem_limit_bytes=VMEM_BYTES
        ),
    )(*[a if a.size == 1 else pltpu.with_memory_space_constraint(a, pltpu.HBM) for a in args])
    return hand_out(*results)


def solution(mesh):
    placed = (
        P(("groups", "row"), "col", None, None, None),
        P(("groups", "row"), "col", None),
        P(("groups", "row"), "col", None),
        P(("groups", "row"), "col"),
        P(("groups", "col", "row"), None),
        P(("groups", "col", "row"), None),
        P(("groups", "row", "col"), None),
        P(("groups", "row", "col"), None),
        P(("groups", "col", "row"), None),
        P(("groups", "col", "row"), None),
        P(("groups", "col", "row"), None),
        P(("groups", "col", "row"), None),
        P(("groups", "row", "col"), None),
        P("groups"),
        P("groups"),
    )
    return jax.shard_map(
        functools.partial(body, mesh.shape["row"]),
        mesh=mesh,
        in_specs=placed,
        out_specs=(
            P(("groups", "row", "col"), None),
            P(("groups", "col", "row"), None),
            P(("groups", "col", "row"), None),
        ),
        check_vma=False,
    )
```

```python
import functools

import jax
import jax.numpy as jnp
from jax import lax
from jax.experimental import pallas as pl
from jax.experimental.pallas import tpu as pltpu
from jax.sharding import PartitionSpec as P

MESH = pl.DeviceIdType.MESH
BLOCK_CHUNKS = 4
FORWARD_GROUPS = ((0, 1, 2, 3), (4, 5), (6, 7))
BACKWARD_GROUPS = ((7, 6), (5, 4), (3, 2, 1, 0))
KX_SLOTS = 16
KTY_SLOTS = 16
VMEM_BYTES = 32 * 1024 * 1024


def kernel(
    n_row,
    blocks,
    block_rows,
    block_cols,
    block_counts,
    primal,
    primal_bar,
    dual,
    rhs,
    cost_vec,
    lower,
    upper,
    bound_kind,
    row_kind,
    primal_step,
    dual_step,
    dual_out,
    primal_out,
    bar_out,
    blk,
    turned,
    placed,
    lane_v,
    order_v,
    order_s,
    pieces_x,
    rows_s,
    cols_s,
    count_s,
    pstep_s,
    dstep_s,
    xall,
    dual_v,
    primal_v,
    kind_row_v,
    kind_v,
    packed,
    part,
    yall,
    kty,
    pieces,
    local_sem,
    order_sem,
    blk_sem,
    x_send,
    x_recv,
    pair_send,
    pair_recv,
    t_send,
    t_recv,
):
    r = lax.axis_index("row")
    c = lax.axis_index("col")
    slots, size = blk.shape[0], blk.shape[1]
    xb = primal.shape[0]
    yb = dual.shape[0]
    mine = pl.ds(pl.multiple_of(r * xb, xb), xb)
    per_chunk = slots // BLOCK_CHUNKS

    def local(src, dst, i):
        copy = pltpu.make_async_copy(src, dst, local_sem.at[i])
        copy.start()
        return copy

    x_copy = local(primal_bar, xall.at[mine], 0)

    def peer(k):
        if n_row > 8:
            return lax.rem(r + k, n_row)
        other = r
        for b in (1, 2, 4):
            if k & b:
                other = other + b * (1 - 2 * lax.rem(r // b, 2))
        return other

    def for_peers(do):
        if n_row <= 8:
            for k in range(n_row - 1, 0, -1):
                do(k)
        else:
            lax.fori_loop(1, n_row, lambda k, carry: (do(k), carry)[1], 0)

    barrier = pltpu.get_barrier_semaphore()
    for_peers(
        lambda k: pl.semaphore_signal(
            barrier, inc=1, device_id={"row": peer(k)}, device_id_type=MESH
        )
    )
    pl.semaphore_signal(barrier, inc=1, device_id={"col": 1 - c}, device_id_type=MESH)

    dual_copies = [
        local(dual, dual_v.at[0], 1),
        local(rhs, dual_v.at[1], 2),
        local(row_kind, kind_row_v, 3),
        local(dual_step, dstep_s, 4),
    ]
    index_copies = [
        local(block_rows.at[0], rows_s, 5),
        local(block_cols.at[0], cols_s, 6),
        local(block_cols.at[0], lane_v.at[0], 14),
        local(block_rows.at[0], lane_v.at[1], 15),
        local(block_counts, count_s, 7),
    ]
    blk_copies = []
    for k in range(BLOCK_CHUNKS):
        span = pl.ds(k * per_chunk, per_chunk)
        copy = pltpu.make_async_copy(blocks.at[0, 0, span], blk.at[span], blk_sem.at[k])
        copy.start()
        blk_copies.append(copy)
    primal_copies = [
        local(primal, primal_v.at[0], 8),
        local(cost_vec, primal_v.at[1], 9),
        local(lower, primal_v.at[2], 10),
        local(upper, primal_v.at[3], 11),
        local(bound_kind, kind_v, 12),
        local(primal_step, pstep_s, 13),
    ]

    pl.semaphore_wait(barrier, n_row)

    def x_remote(k):
        return pltpu.make_async_remote_copy(
            src_ref=xall.at[mine],
            dst_ref=xall.at[mine],
            send_sem=x_send.at[k],
            recv_sem=x_recv.at[k],
            device_id={"row": peer(k)},
            device_id_type=MESH,
        )

    x_copy.wait()
    for_peers(lambda k: x_remote(k).start())

    for copy in dual_copies:
        copy.wait()
    dstep = dstep_s[0]
    packed[c, 0] = dual_v[0] + dstep * dual_v[1]
    packed[c, 1] = jnp.where(kind_row_v[...] == 1, 0.0, -jnp.inf)

    def to_pair(src, dst, i):
        return pltpu.make_async_remote_copy(
            src_ref=src,
            dst_ref=dst,
            send_sem=pair_send.at[i],
            recv_sem=pair_recv.at[i],
            device_id={"col": 1 - c},
            device_id_type=MESH,
        )

    pack_copy = to_pair(packed.at[c], packed.at[c], 0)
    pack_copy.start()

    for copy in index_copies:
        copy.wait()
    count = count_s[0, 0]
    row_iota = lax.broadcasted_iota(jnp.int32, (2 * yb, size), 0)
    col_iota = lax.broadcasted_iota(jnp.int32, (xb * n_row, size), 0)
    by_owner = n_row <= 8
    cap = slots // n_row

    def owner_slots(k):
        return pl.multiple_of(peer(k) * cap, cap) if k else pl.multiple_of(r * cap, cap)

    if by_owner:
        cols_row = lane_v[0]
        here = lax.broadcasted_iota(jnp.int32, (slots, slots), 0)
        lane = lax.broadcasted_iota(jnp.int32, (slots, slots), 1)
        owner = jnp.where(lane[:1] < count, cols_row // xb, -1)
        owner_of = jnp.broadcast_to(owner, (slots, slots)).T
        same = (owner_of == owner) & (here < lane)
        rank = jnp.sum(same.astype(jnp.int32), axis=0, keepdims=True)
        place = jnp.where(owner < 0, -1, owner * cap + rank)
        hit = jnp.broadcast_to(place, (slots, slots)).T == lane
        rows_of = jnp.broadcast_to(lane_v[1], (slots, slots)).T
        inner_of = jnp.broadcast_to(lax.rem(cols_row, xb), (slots, slots)).T

        def placed_at(values):
            return jnp.sum(jnp.where(hit, values, 0), axis=0, keepdims=True)

        full = placed_at(jnp.ones_like(here))
        for i, values in enumerate((here, rows_of, inner_of)):
            order_v[i : i + 1, :] = placed_at(values)
        for i in (1, 2):
            order_v[i + 2 : i + 3, :] = jnp.where(full > 0, order_v[i : i + 1, :], -1)
        order_copy = pltpu.make_async_copy(order_v, order_s, order_sem)
        order_copy.start()
        order_copy.wait()

    def turn(n, carry):
        if by_owner:
            block = blk[order_s[0, n]]
            placed[n] = block
            turned[n] = block.T
        else:
            turned[n] = blk[n].T
        return carry

    for copy in blk_copies:
        copy.wait()
    lax.fori_loop(0, slots, turn, 0, unroll=8)

    inner_iota = lax.broadcasted_iota(jnp.int32, (xb, size), 0)

    def owner_forward(k, acc):
        first = owner_slots(k)
        lefts = []
        for i in range(cap):
            p = first + i
            x_row = pieces_x[pl.ds(k * xb + order_s[2, p], 1), :]
            chosen = row_iota == order_s[3, p]
            lefts.append(jnp.where(chosen, x_row, 0.0).astype(jnp.bfloat16))
        right = turned[pl.ds(first, cap)].reshape(cap * size, size)
        return acc + jnp.dot(
            jnp.concatenate(lefts, 1), right, preferred_element_type=jnp.float32
        )

    def owner_backward(k):
        first = owner_slots(k)
        lefts = []
        for i in range(cap):
            p = first + i
            y_row = yall[pl.ds(order_s[1, p], 1), :]
            chosen = inner_iota == order_s[4, p]
            lefts.append(jnp.where(chosen, y_row, 0.0).astype(jnp.bfloat16))
        right = placed[pl.ds(first, cap)].reshape(cap * size, size)
        return jnp.dot(jnp.concatenate(lefts, 1), right, preferred_element_type=jnp.float32)

    if by_owner:
        total = jnp.zeros((2 * yb, size), jnp.float32)
        for group in FORWARD_GROUPS:
            for k in group:
                if k:
                    x_remote(k).wait_recv()
                theirs = pl.ds(pl.multiple_of((peer(k) if k else r) * xb, xb), xb)
                pieces_x[k * xb : (k + 1) * xb, :] = xall[theirs, :]
            for k in group:
                total = owner_forward(k, total)
    else:
        for_peers(lambda k: x_remote(k).wait_recv())

        def picked(n):
            live_row = jnp.where(n < count, rows_s[0, n], -1)
            return jnp.where(row_iota == live_row, xall[pl.ds(cols_s[0, n], 1), :], 0.0)

        def forward(q, acc):
            n = KX_SLOTS * q
            left = jnp.concatenate([picked(n + i).astype(jnp.bfloat16) for i in range(KX_SLOTS)], 1)
            right = turned[pl.ds(n, KX_SLOTS)].reshape(KX_SLOTS * size, size)
            return acc + jnp.dot(left, right, preferred_element_type=jnp.float32)

        acc = jnp.zeros((2 * yb, size), jnp.float32)
        total = lax.fori_loop(0, slots // KX_SLOTS, forward, acc, unroll=4)
    for h in range(2):
        part[0, h] = total[h * yb : (h + 1) * yb]
    part_copy = to_pair(part.at[0], part.at[1], 1)
    part_copy.start()
    pack_copy.wait_recv()
    part_copy.wait_recv()

    news = []
    for h in range(2):
        moved = packed[h, 0] - dstep * (part[0, h] + part[1, h])
        new = jnp.maximum(moved, packed[h, 1])
        news.append(new)
        yall[h * yb : (h + 1) * yb, :] = new.astype(jnp.bfloat16).astype(jnp.float32)
    dual_out[...] = jnp.where(c == 0, news[0], news[1])

    def masked(n):
        live_col = jnp.where(n < count, cols_s[0, n], -1)
        return jnp.where(col_iota == live_col, yall[pl.ds(rows_s[0, n], 1), :], 0.0)

    def backward(q, acc):
        n = KTY_SLOTS * q
        left = jnp.concatenate([masked(n + i).astype(jnp.bfloat16) for i in range(KTY_SLOTS)], 1)
        right = blk[pl.ds(n, KTY_SLOTS)].reshape(KTY_SLOTS * size, size)
        return acc + jnp.dot(left, right, preferred_element_type=jnp.float32)

    if not by_owner:
        kty[...] = jnp.zeros_like(kty)

        def into(q, carry):
            kty[...] = backward(q, kty[...])
            return carry

        lax.fori_loop(0, slots // KTY_SLOTS, into, 0)

    def t_remote(k):
        at = k if by_owner else peer(k)
        return pltpu.make_async_remote_copy(
            src_ref=kty.at[pl.ds(pl.multiple_of(at * xb, xb), xb)],
            dst_ref=pieces.at[k],
            send_sem=t_send.at[k],
            recv_sem=t_recv.at[k],
            device_id={"row": peer(k)},
            device_id_type=MESH,
        )

    if by_owner:
        for group in BACKWARD_GROUPS:
            sums = [owner_backward(k) for k in group]
            for k, part_sum in zip(group, sums):
                if k:
                    kty[k * xb : (k + 1) * xb, :] = part_sum
                    t_remote(k).start()
                else:
                    total = part_sum
    else:
        for_peers(lambda k: t_remote(k).start())
        total = kty[mine, :]
    for copy in primal_copies:
        copy.wait()
    if by_owner:
        for k in range(1, n_row):
            t_remote(k).wait_recv()
            total = total + pieces[k]
    else:
        for_peers(lambda k: t_remote(k).wait_recv())
        total = lax.fori_loop(1, n_row, lambda k, s: s + pieces[k], total)

    old = primal_v[0]
    kind = kind_v[...]
    moved = old - pstep_s[0] * (primal_v[1] - total)
    moved = jnp.where((kind == 1) | (kind == 3), jnp.maximum(moved, primal_v[2]), moved)
    new = jnp.where((kind == 2) | (kind == 3), jnp.minimum(moved, primal_v[3]), moved)
    primal_out[...] = new
    bar_out[...] = 2.0 * new - old

    for_peers(lambda k: x_remote(k).wait_send())
    pack_copy.wait_send()
    part_copy.wait_send()
    for_peers(lambda k: t_remote(k).wait_send())


def hand_out_kernel(dual_v, primal_v, bar_v, dual_out, primal_out, bar_out, sem):
    copies = [
        pltpu.make_async_copy(src, dst, sem.at[i])
        for i, (src, dst) in enumerate(
            ((dual_v, dual_out), (primal_v, primal_out), (bar_v, bar_out))
        )
    ]
    for copy in copies:
        copy.start()
    for copy in copies:
        copy.wait()


def hand_out(*results):
    return pl.pallas_call(
        hand_out_kernel,
        out_shape=tuple(jax.ShapeDtypeStruct(a.shape, a.dtype) for a in results),
        in_specs=[pl.BlockSpec(memory_space=pltpu.VMEM)] * 3,
        out_specs=[pl.BlockSpec(memory_space=pltpu.HBM)] * 3,
        scratch_shapes=[pltpu.SemaphoreType.DMA((3,))],
        compiler_params=pltpu.CompilerParams(vmem_limit_bytes=VMEM_BYTES),
    )(*results)


def body(n_row, *args):
    blocks, block_rows, primal, dual = args[0], args[1], args[4], args[6]
    slots, size = blocks.shape[2], blocks.shape[3]
    xb, yb = primal.shape[0], dual.shape[0]
    f32, i32 = jnp.float32, jnp.int32
    dma = pltpu.SemaphoreType.DMA
    results = pl.pallas_call(
        functools.partial(kernel, n_row),
        out_shape=(
            pltpu.VMEM((yb, size), f32),
            pltpu.VMEM((xb, size), f32),
            pltpu.VMEM((xb, size), f32),
        ),
        in_specs=[pl.BlockSpec(memory_space=pltpu.HBM)] * len(args),
        out_specs=[pl.BlockSpec(memory_space=pltpu.VMEM)] * 3,
        scratch_shapes=[
            pltpu.VMEM((slots, size, size), jnp.bfloat16),
            pltpu.VMEM((slots, size, size), jnp.bfloat16),
            pltpu.VMEM((slots, size, size), jnp.bfloat16),
            pltpu.VMEM((2, 1, slots), i32),
            pltpu.VMEM((8, slots), i32),
            pltpu.SMEM((8, slots), i32),
            pltpu.VMEM((n_row * xb, size), f32),
            pltpu.SMEM((1, slots), i32),
            pltpu.SMEM((1, slots), i32),
            pltpu.SMEM((1, 1), i32),
            pltpu.SMEM((1,), f32),
            pltpu.SMEM((1,), f32),
            pltpu.VMEM((n_row * xb, size), f32),
            pltpu.VMEM((2, yb, size), f32),
            pltpu.VMEM((4, xb, size), f32),
            pltpu.VMEM((yb, size), i32),
            pltpu.VMEM((xb, size), i32),
            pltpu.VMEM((2, 2, yb, size), f32),
            pltpu.VMEM((2, 2, yb, size), f32),
            pltpu.VMEM((2 * yb, size), f32),
            pltpu.VMEM((n_row * xb, size), f32),
            pltpu.VMEM((n_row, xb, size), f32),
            dma((16,)),
            dma(()),
            dma((BLOCK_CHUNKS,)),
            dma((n_row,)),
            dma((n_row,)),
            dma((2,)),
            dma((2,)),
            dma((n_row,)),
            dma((n_row,)),
        ],
        compiler_params=pltpu.CompilerParams(
            collective_id=0, has_side_effects=True, vmem_limit_bytes=VMEM_BYTES
        ),
    )(*[a if a.size == 1 else pltpu.with_memory_space_constraint(a, pltpu.HBM) for a in args])
    return hand_out(*results)


def solution(mesh):
    placed = (
        P(("groups", "row"), "col", None, None, None),
        P(("groups", "row"), "col", None),
        P(("groups", "row"), "col", None),
        P(("groups", "row"), "col"),
        P(("groups", "col", "row"), None),
        P(("groups", "col", "row"), None),
        P(("groups", "row", "col"), None),
        P(("groups", "row", "col"), None),
        P(("groups", "col", "row"), None),
        P(("groups", "col", "row"), None),
        P(("groups", "col", "row"), None),
        P(("groups", "col", "row"), None),
        P(("groups", "row", "col"), None),
        P("groups"),
        P("groups"),
    )
    return jax.shard_map(
        functools.partial(body, mesh.shape["row"]),
        mesh=mesh,
        in_specs=placed,
        out_specs=(
            P(("groups", "row", "col"), None),
            P(("groups", "col", "row"), None),
            P(("groups", "col", "row"), None),
        ),
        check_vma=False,
    )
```

```python
import functools

import jax
import jax.numpy as jnp
from jax import lax
from jax.experimental import pallas as pl
from jax.experimental.pallas import tpu as pltpu
from jax.sharding import PartitionSpec as P

MESH = pl.DeviceIdType.MESH
BLOCK_CHUNKS = 4
FORWARD_GROUPS = ((0, 1, 2, 3), (4, 5), (6,), (7,))
BACKWARD_GROUPS = ((7,), (6,), (5, 4), (3, 2, 1, 0))
KX_SLOTS = 16
KTY_SLOTS = 16
VMEM_BYTES = 32 * 1024 * 1024


def kernel(
    n_row,
    blocks,
    block_rows,
    block_cols,
    block_counts,
    primal,
    primal_bar,
    dual,
    rhs,
    cost_vec,
    lower,
    upper,
    bound_kind,
    row_kind,
    primal_step,
    dual_step,
    dual_out,
    primal_out,
    bar_out,
    blk,
    turned,
    placed,
    lane_v,
    order_v,
    order_s,
    pieces_x,
    rows_s,
    cols_s,
    xall,
    dual_v,
    primal_v,
    kind_row_v,
    kind_v,
    packed,
    part,
    yall,
    kty,
    pieces,
    local_sem,
    order_sem,
    blk_sem,
    x_send,
    x_recv,
    pair_send,
    pair_recv,
    t_send,
    t_recv,
):
    r = lax.axis_index("row")
    c = lax.axis_index("col")
    slots, size = blk.shape[0], blk.shape[1]
    xb = primal.shape[0]
    yb = dual.shape[0]
    mine = pl.ds(pl.multiple_of(r * xb, xb), xb)
    per_chunk = slots // BLOCK_CHUNKS

    def local(src, dst, i):
        copy = pltpu.make_async_copy(src, dst, local_sem.at[i])
        copy.start()
        return copy

    x_copy = local(primal_bar, xall.at[mine], 0)

    def peer(k):
        if n_row > 8:
            return lax.rem(r + k, n_row)
        other = r
        for b in (1, 2, 4):
            if k & b:
                other = other + b * (1 - 2 * lax.rem(r // b, 2))
        return other

    def for_peers(do):
        if n_row <= 8:
            for k in range(n_row - 1, 0, -1):
                do(k)
        else:
            lax.fori_loop(1, n_row, lambda k, carry: (do(k), carry)[1], 0)

    barrier = pltpu.get_barrier_semaphore()
    for_peers(
        lambda k: pl.semaphore_signal(
            barrier, inc=1, device_id={"row": peer(k)}, device_id_type=MESH
        )
    )
    pl.semaphore_signal(barrier, inc=1, device_id={"col": 1 - c}, device_id_type=MESH)

    dual_copies = [
        local(dual, dual_v.at[0], 1),
        local(rhs, dual_v.at[1], 2),
        local(row_kind, kind_row_v, 3),
    ]
    index_copies = [
        local(block_cols.at[0], lane_v.at[0] if n_row <= 8 else cols_s, 5),
        local(block_rows.at[0], lane_v.at[1] if n_row <= 8 else rows_s, 6),
    ]
    blk_copies = []
    for k in range(BLOCK_CHUNKS):
        span = pl.ds(k * per_chunk, per_chunk)
        copy = pltpu.make_async_copy(blocks.at[0, 0, span], blk.at[span], blk_sem.at[k])
        copy.start()
        blk_copies.append(copy)
    primal_copies = [
        local(primal, primal_v.at[0], 8),
        local(cost_vec, primal_v.at[1], 9),
        local(lower, primal_v.at[2], 10),
        local(upper, primal_v.at[3], 11),
        local(bound_kind, kind_v, 12),
    ]

    pl.semaphore_wait(barrier, n_row)

    def x_remote(k):
        return pltpu.make_async_remote_copy(
            src_ref=xall.at[mine],
            dst_ref=xall.at[mine],
            send_sem=x_send.at[k],
            recv_sem=x_recv.at[k],
            device_id={"row": peer(k)},
            device_id_type=MESH,
        )

    x_copy.wait()
    for_peers(lambda k: x_remote(k).start())

    for copy in dual_copies:
        copy.wait()
    dstep = dual_step[0]
    packed[c, 0] = dual_v[0] + dstep * dual_v[1]
    packed[c, 1] = jnp.where(kind_row_v[...] == 1, 0.0, -jnp.inf)

    def to_pair(src, dst, i):
        return pltpu.make_async_remote_copy(
            src_ref=src,
            dst_ref=dst,
            send_sem=pair_send.at[i],
            recv_sem=pair_recv.at[i],
            device_id={"col": 1 - c},
            device_id_type=MESH,
        )

    pack_copy = to_pair(packed.at[c], packed.at[c], 0)
    pack_copy.start()

    for copy in index_copies:
        copy.wait()
    count = block_counts[0, 0]
    row_iota = lax.broadcasted_iota(jnp.int32, (2 * yb, size), 0)
    col_iota = lax.broadcasted_iota(jnp.int32, (xb * n_row, size), 0)
    by_owner = n_row <= 8
    cap = slots // n_row

    def owner_slots(k):
        return pl.multiple_of(peer(k) * cap, cap) if k else pl.multiple_of(r * cap, cap)

    if by_owner:
        cols_row = lane_v[0]
        here = lax.broadcasted_iota(jnp.int32, (slots, slots), 0)
        lane = lax.broadcasted_iota(jnp.int32, (slots, slots), 1)
        owner = jnp.where(lane[:1] < count, cols_row // xb, -1)
        owner_of = jnp.broadcast_to(owner, (slots, slots)).T
        same = (owner_of == owner) & (here < lane)
        rank = jnp.sum(same.astype(jnp.int32), axis=0, keepdims=True)
        place = jnp.where(owner < 0, -1, owner * cap + rank)
        hit = jnp.broadcast_to(place, (slots, slots)).T == lane
        rows_of = jnp.broadcast_to(lane_v[1], (slots, slots)).T
        inner_of = jnp.broadcast_to(lax.rem(cols_row, xb), (slots, slots)).T

        def placed_at(values):
            return jnp.sum(jnp.where(hit, values, 0), axis=0, keepdims=True)

        full = placed_at(jnp.ones_like(here))
        for i, values in enumerate((here, rows_of, inner_of)):
            order_v[i : i + 1, :] = placed_at(values)
        for i in (1, 2):
            order_v[i + 2 : i + 3, :] = jnp.where(full > 0, order_v[i : i + 1, :], -1)
        order_copy = pltpu.make_async_copy(order_v, order_s, order_sem)
        order_copy.start()
        order_copy.wait()

    def turn(n, carry):
        if by_owner:
            block = blk[order_s[0, n]]
            placed[n] = block
            turned[n] = block.T
        else:
            turned[n] = blk[n].T
        return carry

    for copy in blk_copies:
        copy.wait()
    lax.fori_loop(0, slots, turn, 0, unroll=8)

    inner_iota = lax.broadcasted_iota(jnp.int32, (xb, size), 0)

    def owner_forward(k, acc):
        first = owner_slots(k)
        lefts = []
        for i in range(cap):
            p = first + i
            x_row = pieces_x[pl.ds(k * xb + order_s[2, p], 1), :]
            chosen = row_iota == order_s[3, p]
            lefts.append(jnp.where(chosen, x_row, 0.0).astype(jnp.bfloat16))
        right = turned[pl.ds(first, cap)].reshape(cap * size, size)
        return acc + jnp.dot(
            jnp.concatenate(lefts, 1), right, preferred_element_type=jnp.float32
        )

    def owner_backward(k):
        first = owner_slots(k)
        lefts = []
        for i in range(cap):
            p = first + i
            y_row = yall[pl.ds(order_s[1, p], 1), :]
            chosen = inner_iota == order_s[4, p]
            lefts.append(jnp.where(chosen, y_row, 0.0).astype(jnp.bfloat16))
        right = placed[pl.ds(first, cap)].reshape(cap * size, size)
        return jnp.dot(jnp.concatenate(lefts, 1), right, preferred_element_type=jnp.float32)

    if by_owner:
        total = jnp.zeros((2 * yb, size), jnp.float32)
        for group in FORWARD_GROUPS:
            for k in group:
                if k:
                    x_remote(k).wait_recv()
                theirs = pl.ds(pl.multiple_of((peer(k) if k else r) * xb, xb), xb)
                pieces_x[k * xb : (k + 1) * xb, :] = xall[theirs, :]
            for k in group:
                total = owner_forward(k, total)
    else:
        for_peers(lambda k: x_remote(k).wait_recv())

        def picked(n):
            live_row = jnp.where(n < count, rows_s[0, n], -1)
            return jnp.where(row_iota == live_row, xall[pl.ds(cols_s[0, n], 1), :], 0.0)

        def forward(q, acc):
            n = KX_SLOTS * q
            left = jnp.concatenate([picked(n + i).astype(jnp.bfloat16) for i in range(KX_SLOTS)], 1)
            right = turned[pl.ds(n, KX_SLOTS)].reshape(KX_SLOTS * size, size)
            return acc + jnp.dot(left, right, preferred_element_type=jnp.float32)

        acc = jnp.zeros((2 * yb, size), jnp.float32)
        total = lax.fori_loop(0, slots // KX_SLOTS, forward, acc, unroll=4)
    for h in range(2):
        part[0, h] = total[h * yb : (h + 1) * yb]
    part_copy = to_pair(part.at[0], part.at[1], 1)
    part_copy.start()
    pack_copy.wait_recv()
    part_copy.wait_recv()

    news = []
    for h in range(2):
        moved = packed[h, 0] - dstep * (part[0, h] + part[1, h])
        new = jnp.maximum(moved, packed[h, 1])
        news.append(new)
        yall[h * yb : (h + 1) * yb, :] = new.astype(jnp.bfloat16).astype(jnp.float32)
    dual_out[...] = jnp.where(c == 0, news[0], news[1])

    def masked(n):
        live_col = jnp.where(n < count, cols_s[0, n], -1)
        return jnp.where(col_iota == live_col, yall[pl.ds(rows_s[0, n], 1), :], 0.0)

    def backward(q, acc):
        n = KTY_SLOTS * q
        left = jnp.concatenate([masked(n + i).astype(jnp.bfloat16) for i in range(KTY_SLOTS)], 1)
        right = blk[pl.ds(n, KTY_SLOTS)].reshape(KTY_SLOTS * size, size)
        return acc + jnp.dot(left, right, preferred_element_type=jnp.float32)

    if not by_owner:
        kty[...] = jnp.zeros_like(kty)

        def into(q, carry):
            kty[...] = backward(q, kty[...])
            return carry

        lax.fori_loop(0, slots // KTY_SLOTS, into, 0)

    def t_remote(k):
        at = k if by_owner else peer(k)
        return pltpu.make_async_remote_copy(
            src_ref=kty.at[pl.ds(pl.multiple_of(at * xb, xb), xb)],
            dst_ref=pieces.at[k],
            send_sem=t_send.at[k],
            recv_sem=t_recv.at[k],
            device_id={"row": peer(k)},
            device_id_type=MESH,
        )

    if by_owner:
        for group in BACKWARD_GROUPS:
            sums = [owner_backward(k) for k in group]
            for k, part_sum in zip(group, sums):
                if k:
                    kty[k * xb : (k + 1) * xb, :] = part_sum
                    t_remote(k).start()
                else:
                    total = part_sum
    else:
        for_peers(lambda k: t_remote(k).start())
        total = kty[mine, :]
    for copy in primal_copies:
        copy.wait()
    if by_owner:
        for k in range(1, n_row):
            t_remote(k).wait_recv()
            total = total + pieces[k]
    else:
        for_peers(lambda k: t_remote(k).wait_recv())
        total = lax.fori_loop(1, n_row, lambda k, s: s + pieces[k], total)

    old = primal_v[0]
    kind = kind_v[...]
    moved = old - primal_step[0] * (primal_v[1] - total)
    moved = jnp.where((kind == 1) | (kind == 3), jnp.maximum(moved, primal_v[2]), moved)
    new = jnp.where((kind == 2) | (kind == 3), jnp.minimum(moved, primal_v[3]), moved)
    primal_out[...] = new
    bar_out[...] = 2.0 * new - old

    for_peers(lambda k: x_remote(k).wait_send())
    pack_copy.wait_send()
    part_copy.wait_send()
    for_peers(lambda k: t_remote(k).wait_send())


def hand_out_kernel(dual_v, primal_v, bar_v, dual_out, primal_out, bar_out, sem):
    copies = [
        pltpu.make_async_copy(src, dst, sem.at[i])
        for i, (src, dst) in enumerate(
            ((dual_v, dual_out), (primal_v, primal_out), (bar_v, bar_out))
        )
    ]
    for copy in copies:
        copy.start()
    for copy in copies:
        copy.wait()


def hand_out(*results):
    return pl.pallas_call(
        hand_out_kernel,
        out_shape=tuple(jax.ShapeDtypeStruct(a.shape, a.dtype) for a in results),
        in_specs=[pl.BlockSpec(memory_space=pltpu.VMEM)] * 3,
        out_specs=[pl.BlockSpec(memory_space=pltpu.HBM)] * 3,
        scratch_shapes=[pltpu.SemaphoreType.DMA((3,))],
        compiler_params=pltpu.CompilerParams(vmem_limit_bytes=VMEM_BYTES),
    )(*results)


def body(n_row, *args):
    blocks, block_rows, primal, dual = args[0], args[1], args[4], args[6]
    slots, size = blocks.shape[2], blocks.shape[3]
    xb, yb = primal.shape[0], dual.shape[0]
    f32, i32 = jnp.float32, jnp.int32
    dma = pltpu.SemaphoreType.DMA
    results = pl.pallas_call(
        functools.partial(kernel, n_row),
        out_shape=(
            pltpu.VMEM((yb, size), f32),
            pltpu.VMEM((xb, size), f32),
            pltpu.VMEM((xb, size), f32),
        ),
        in_specs=[
            pl.BlockSpec(memory_space=pltpu.SMEM if a.size == 1 else pltpu.HBM) for a in args
        ],
        out_specs=[pl.BlockSpec(memory_space=pltpu.VMEM)] * 3,
        scratch_shapes=[
            pltpu.VMEM((slots, size, size), jnp.bfloat16),
            pltpu.VMEM((slots, size, size), jnp.bfloat16),
            pltpu.VMEM((slots, size, size), jnp.bfloat16),
            pltpu.VMEM((2, 1, slots), i32),
            pltpu.VMEM((8, slots), i32),
            pltpu.SMEM((8, slots), i32),
            pltpu.VMEM((n_row * xb, size), f32),
            pltpu.SMEM((1, slots), i32),
            pltpu.SMEM((1, slots), i32),
            pltpu.VMEM((n_row * xb, size), f32),
            pltpu.VMEM((2, yb, size), f32),
            pltpu.VMEM((4, xb, size), f32),
            pltpu.VMEM((yb, size), i32),
            pltpu.VMEM((xb, size), i32),
            pltpu.VMEM((2, 2, yb, size), f32),
            pltpu.VMEM((2, 2, yb, size), f32),
            pltpu.VMEM((2 * yb, size), f32),
            pltpu.VMEM((n_row * xb, size), f32),
            pltpu.VMEM((n_row, xb, size), f32),
            dma((16,)),
            dma(()),
            dma((BLOCK_CHUNKS,)),
            dma((n_row,)),
            dma((n_row,)),
            dma((2,)),
            dma((2,)),
            dma((n_row,)),
            dma((n_row,)),
        ],
        compiler_params=pltpu.CompilerParams(
            collective_id=0, has_side_effects=True, vmem_limit_bytes=VMEM_BYTES
        ),
    )(*[a if a.size == 1 else pltpu.with_memory_space_constraint(a, pltpu.HBM) for a in args])
    return hand_out(*results)


def solution(mesh):
    placed = (
        P(("groups", "row"), "col", None, None, None),
        P(("groups", "row"), "col", None),
        P(("groups", "row"), "col", None),
        P(("groups", "row"), "col"),
        P(("groups", "col", "row"), None),
        P(("groups", "col", "row"), None),
        P(("groups", "row", "col"), None),
        P(("groups", "row", "col"), None),
        P(("groups", "col", "row"), None),
        P(("groups", "col", "row"), None),
        P(("groups", "col", "row"), None),
        P(("groups", "col", "row"), None),
        P(("groups", "row", "col"), None),
        P("groups"),
        P("groups"),
    )
    return jax.shard_map(
        functools.partial(body, mesh.shape["row"]),
        mesh=mesh,
        in_specs=placed,
        out_specs=(
            P(("groups", "row", "col"), None),
            P(("groups", "col", "row"), None),
            P(("groups", "col", "row"), None),
        ),
        check_vma=False,
    )
```

```python
import functools

import jax
import jax.numpy as jnp
from jax import lax
from jax.experimental import pallas as pl
from jax.experimental.pallas import tpu as pltpu
from jax.sharding import PartitionSpec as P

MESH = pl.DeviceIdType.MESH
BLOCK_CHUNKS = 4
FORWARD_GROUPS = ((0, 1), (2, 3), (4, 5), (6,), (7,))
BACKWARD_GROUPS = ((7, 6), (5, 4), (3, 2, 1, 0))
KX_SLOTS = 16
KTY_SLOTS = 16
VMEM_BYTES = 32 * 1024 * 1024


def kernel(
    n_row,
    blocks,
    block_rows,
    block_cols,
    block_counts,
    primal,
    primal_bar,
    dual,
    rhs,
    cost_vec,
    lower,
    upper,
    bound_kind,
    row_kind,
    primal_step,
    dual_step,
    dual_out,
    primal_out,
    bar_out,
    blk,
    turned,
    placed,
    lane_v,
    order_v,
    order_s,
    pieces_x,
    rows_s,
    cols_s,
    count_s,
    pstep_s,
    dstep_s,
    xall,
    dual_v,
    primal_v,
    kind_row_v,
    kind_v,
    packed,
    part,
    yall,
    kty,
    pieces,
    local_sem,
    order_sem,
    blk_sem,
    x_send,
    x_recv,
    pair_send,
    pair_recv,
    t_send,
    t_recv,
):
    r = lax.axis_index("row")
    c = lax.axis_index("col")
    slots, size = blk.shape[0], blk.shape[1]
    xb = primal.shape[0]
    yb = dual.shape[0]
    mine = pl.ds(pl.multiple_of(r * xb, xb), xb)
    per_chunk = slots // BLOCK_CHUNKS

    def local(src, dst, i):
        copy = pltpu.make_async_copy(src, dst, local_sem.at[i])
        copy.start()
        return copy

    x_copy = local(primal_bar, xall.at[mine], 0)

    def peer(k):
        if n_row > 8:
            return lax.rem(r + k, n_row)
        other = r
        for b in (1, 2, 4):
            if k & b:
                other = other + b * (1 - 2 * lax.rem(r // b, 2))
        return other

    def for_peers(do):
        if n_row <= 8:
            for k in range(n_row - 1, 0, -1):
                do(k)
        else:
            lax.fori_loop(1, n_row, lambda k, carry: (do(k), carry)[1], 0)

    barrier = pltpu.get_barrier_semaphore()
    for_peers(
        lambda k: pl.semaphore_signal(
            barrier, inc=1, device_id={"row": peer(k)}, device_id_type=MESH
        )
    )
    pl.semaphore_signal(barrier, inc=1, device_id={"col": 1 - c}, device_id_type=MESH)

    dual_copies = [
        local(dual, dual_v.at[0], 1),
        local(rhs, dual_v.at[1], 2),
        local(row_kind, kind_row_v, 3),
        local(dual_step, dstep_s, 4),
    ]
    index_copies = [
        local(block_rows.at[0], rows_s, 5),
        local(block_cols.at[0], cols_s, 6),
        local(block_cols.at[0], lane_v.at[0], 14),
        local(block_rows.at[0], lane_v.at[1], 15),
        local(block_counts, count_s, 7),
    ]
    blk_copies = []
    for k in range(BLOCK_CHUNKS):
        span = pl.ds(k * per_chunk, per_chunk)
        copy = pltpu.make_async_copy(blocks.at[0, 0, span], blk.at[span], blk_sem.at[k])
        copy.start()
        blk_copies.append(copy)
    primal_copies = [
        local(primal, primal_v.at[0], 8),
        local(cost_vec, primal_v.at[1], 9),
        local(lower, primal_v.at[2], 10),
        local(upper, primal_v.at[3], 11),
        local(bound_kind, kind_v, 12),
        local(primal_step, pstep_s, 13),
    ]

    pl.semaphore_wait(barrier, n_row)

    def x_remote(k):
        return pltpu.make_async_remote_copy(
            src_ref=xall.at[mine],
            dst_ref=xall.at[mine],
            send_sem=x_send.at[k],
            recv_sem=x_recv.at[k],
            device_id={"row": peer(k)},
            device_id_type=MESH,
        )

    x_copy.wait()
    for_peers(lambda k: x_remote(k).start())

    for copy in dual_copies:
        copy.wait()
    dstep = dstep_s[0]
    packed[c, 0] = dual_v[0] + dstep * dual_v[1]
    packed[c, 1] = jnp.where(kind_row_v[...] == 1, 0.0, -jnp.inf)

    def to_pair(src, dst, i):
        return pltpu.make_async_remote_copy(
            src_ref=src,
            dst_ref=dst,
            send_sem=pair_send.at[i],
            recv_sem=pair_recv.at[i],
            device_id={"col": 1 - c},
            device_id_type=MESH,
        )

    pack_copy = to_pair(packed.at[c], packed.at[c], 0)
    pack_copy.start()

    for copy in index_copies:
        copy.wait()
    count = count_s[0, 0]
    row_iota = lax.broadcasted_iota(jnp.int32, (2 * yb, size), 0)
    col_iota = lax.broadcasted_iota(jnp.int32, (xb * n_row, size), 0)
    by_owner = n_row <= 8
    cap = slots // n_row

    def owner_slots(k):
        return pl.multiple_of(peer(k) * cap, cap) if k else pl.multiple_of(r * cap, cap)

    if by_owner:
        cols_row = lane_v[0]
        here = lax.broadcasted_iota(jnp.int32, (slots, slots), 0)
        lane = lax.broadcasted_iota(jnp.int32, (slots, slots), 1)
        owner = jnp.where(lane[:1] < count, cols_row // xb, -1)
        owner_of = jnp.broadcast_to(owner, (slots, slots)).T
        same = (owner_of == owner) & (here < lane)
        rank = jnp.sum(same.astype(jnp.int32), axis=0, keepdims=True)
        place = jnp.where(owner < 0, -1, owner * cap + rank)
        hit = jnp.broadcast_to(place, (slots, slots)).T == lane
        rows_of = jnp.broadcast_to(lane_v[1], (slots, slots)).T
        inner_of = jnp.broadcast_to(lax.rem(cols_row, xb), (slots, slots)).T

        def placed_at(values):
            return jnp.sum(jnp.where(hit, values, 0), axis=0, keepdims=True)

        full = placed_at(jnp.ones_like(here))
        for i, values in enumerate((here, rows_of, inner_of)):
            order_v[i : i + 1, :] = placed_at(values)
        for i in (1, 2):
            order_v[i + 2 : i + 3, :] = jnp.where(full > 0, order_v[i : i + 1, :], -1)
        order_copy = pltpu.make_async_copy(order_v, order_s, order_sem)
        order_copy.start()
        order_copy.wait()

    def turn(n, carry):
        if by_owner:
            block = blk[order_s[0, n]]
            placed[n] = block
            turned[n] = block.T
        else:
            turned[n] = blk[n].T
        return carry

    for copy in blk_copies:
        copy.wait()
    lax.fori_loop(0, slots, turn, 0, unroll=8)

    inner_iota = lax.broadcasted_iota(jnp.int32, (xb, size), 0)

    def owner_forward(k, acc):
        first = owner_slots(k)
        lefts = []
        for i in range(cap):
            p = first + i
            x_row = pieces_x[pl.ds(k * xb + order_s[2, p], 1), :]
            chosen = row_iota == order_s[3, p]
            lefts.append(jnp.where(chosen, x_row, 0.0).astype(jnp.bfloat16))
        right = turned[pl.ds(first, cap)].reshape(cap * size, size)
        return acc + jnp.dot(
            jnp.concatenate(lefts, 1), right, preferred_element_type=jnp.float32
        )

    def owner_backward(k):
        first = owner_slots(k)
        lefts = []
        for i in range(cap):
            p = first + i
            y_row = yall[pl.ds(order_s[1, p], 1), :]
            chosen = inner_iota == order_s[4, p]
            lefts.append(jnp.where(chosen, y_row, 0.0).astype(jnp.bfloat16))
        right = placed[pl.ds(first, cap)].reshape(cap * size, size)
        return jnp.dot(jnp.concatenate(lefts, 1), right, preferred_element_type=jnp.float32)

    if by_owner:
        total = jnp.zeros((2 * yb, size), jnp.float32)
        for group in FORWARD_GROUPS:
            for k in group:
                if k:
                    x_remote(k).wait_recv()
                theirs = pl.ds(pl.multiple_of((peer(k) if k else r) * xb, xb), xb)
                pieces_x[k * xb : (k + 1) * xb, :] = xall[theirs, :]
            for k in group:
                total = owner_forward(k, total)
    else:
        for_peers(lambda k: x_remote(k).wait_recv())

        def picked(n):
            live_row = jnp.where(n < count, rows_s[0, n], -1)
            return jnp.where(row_iota == live_row, xall[pl.ds(cols_s[0, n], 1), :], 0.0)

        def forward(q, acc):
            n = KX_SLOTS * q
            left = jnp.concatenate([picked(n + i).astype(jnp.bfloat16) for i in range(KX_SLOTS)], 1)
            right = turned[pl.ds(n, KX_SLOTS)].reshape(KX_SLOTS * size, size)
            return acc + jnp.dot(left, right, preferred_element_type=jnp.float32)

        acc = jnp.zeros((2 * yb, size), jnp.float32)
        total = lax.fori_loop(0, slots // KX_SLOTS, forward, acc, unroll=4)
    for h in range(2):
        part[0, h] = total[h * yb : (h + 1) * yb]
    part_copy = to_pair(part.at[0], part.at[1], 1)
    part_copy.start()
    pack_copy.wait_recv()
    part_copy.wait_recv()

    news = []
    for h in range(2):
        moved = packed[h, 0] - dstep * (part[0, h] + part[1, h])
        new = jnp.maximum(moved, packed[h, 1])
        news.append(new)
        yall[h * yb : (h + 1) * yb, :] = new.astype(jnp.bfloat16).astype(jnp.float32)
    dual_out[...] = jnp.where(c == 0, news[0], news[1])

    def masked(n):
        live_col = jnp.where(n < count, cols_s[0, n], -1)
        return jnp.where(col_iota == live_col, yall[pl.ds(rows_s[0, n], 1), :], 0.0)

    def backward(q, acc):
        n = KTY_SLOTS * q
        left = jnp.concatenate([masked(n + i).astype(jnp.bfloat16) for i in range(KTY_SLOTS)], 1)
        right = blk[pl.ds(n, KTY_SLOTS)].reshape(KTY_SLOTS * size, size)
        return acc + jnp.dot(left, right, preferred_element_type=jnp.float32)

    if not by_owner:
        kty[...] = jnp.zeros_like(kty)

        def into(q, carry):
            kty[...] = backward(q, kty[...])
            return carry

        lax.fori_loop(0, slots // KTY_SLOTS, into, 0)

    def t_remote(k):
        at = k if by_owner else peer(k)
        return pltpu.make_async_remote_copy(
            src_ref=kty.at[pl.ds(pl.multiple_of(at * xb, xb), xb)],
            dst_ref=pieces.at[k],
            send_sem=t_send.at[k],
            recv_sem=t_recv.at[k],
            device_id={"row": peer(k)},
            device_id_type=MESH,
        )

    if by_owner:
        for group in BACKWARD_GROUPS:
            sums = [owner_backward(k) for k in group]
            for k, part_sum in zip(group, sums):
                if k:
                    kty[k * xb : (k + 1) * xb, :] = part_sum
                    t_remote(k).start()
                else:
                    total = part_sum
    else:
        for_peers(lambda k: t_remote(k).start())
        total = kty[mine, :]
    for copy in primal_copies:
        copy.wait()
    if by_owner:
        for k in range(1, n_row):
            t_remote(k).wait_recv()
            total = total + pieces[k]
    else:
        for_peers(lambda k: t_remote(k).wait_recv())
        total = lax.fori_loop(1, n_row, lambda k, s: s + pieces[k], total)

    old = primal_v[0]
    kind = kind_v[...]
    moved = old - pstep_s[0] * (primal_v[1] - total)
    moved = jnp.where((kind == 1) | (kind == 3), jnp.maximum(moved, primal_v[2]), moved)
    new = jnp.where((kind == 2) | (kind == 3), jnp.minimum(moved, primal_v[3]), moved)
    primal_out[...] = new
    bar_out[...] = 2.0 * new - old

    for_peers(lambda k: x_remote(k).wait_send())
    pack_copy.wait_send()
    part_copy.wait_send()
    for_peers(lambda k: t_remote(k).wait_send())


def hand_out_kernel(dual_v, primal_v, bar_v, dual_out, primal_out, bar_out, sem):
    copies = [
        pltpu.make_async_copy(src, dst, sem.at[i])
        for i, (src, dst) in enumerate(
            ((dual_v, dual_out), (primal_v, primal_out), (bar_v, bar_out))
        )
    ]
    for copy in copies:
        copy.start()
    for copy in copies:
        copy.wait()


def hand_out(*results):
    return pl.pallas_call(
        hand_out_kernel,
        out_shape=tuple(jax.ShapeDtypeStruct(a.shape, a.dtype) for a in results),
        in_specs=[pl.BlockSpec(memory_space=pltpu.VMEM)] * 3,
        out_specs=[pl.BlockSpec(memory_space=pltpu.HBM)] * 3,
        scratch_shapes=[pltpu.SemaphoreType.DMA((3,))],
        compiler_params=pltpu.CompilerParams(vmem_limit_bytes=VMEM_BYTES),
    )(*results)


def body(n_row, *args):
    blocks, block_rows, primal, dual = args[0], args[1], args[4], args[6]
    slots, size = blocks.shape[2], blocks.shape[3]
    xb, yb = primal.shape[0], dual.shape[0]
    f32, i32 = jnp.float32, jnp.int32
    dma = pltpu.SemaphoreType.DMA
    results = pl.pallas_call(
        functools.partial(kernel, n_row),
        out_shape=(
            pltpu.VMEM((yb, size), f32),
            pltpu.VMEM((xb, size), f32),
            pltpu.VMEM((xb, size), f32),
        ),
        in_specs=[pl.BlockSpec(memory_space=pltpu.HBM)] * len(args),
        out_specs=[pl.BlockSpec(memory_space=pltpu.VMEM)] * 3,
        scratch_shapes=[
            pltpu.VMEM((slots, size, size), jnp.bfloat16),
            pltpu.VMEM((slots, size, size), jnp.bfloat16),
            pltpu.VMEM((slots, size, size), jnp.bfloat16),
            pltpu.VMEM((2, 1, slots), i32),
            pltpu.VMEM((8, slots), i32),
            pltpu.SMEM((8, slots), i32),
            pltpu.VMEM((n_row * xb, size), f32),
            pltpu.SMEM((1, slots), i32),
            pltpu.SMEM((1, slots), i32),
            pltpu.SMEM((1, 1), i32),
            pltpu.SMEM((1,), f32),
            pltpu.SMEM((1,), f32),
            pltpu.VMEM((n_row * xb, size), f32),
            pltpu.VMEM((2, yb, size), f32),
            pltpu.VMEM((4, xb, size), f32),
            pltpu.VMEM((yb, size), i32),
            pltpu.VMEM((xb, size), i32),
            pltpu.VMEM((2, 2, yb, size), f32),
            pltpu.VMEM((2, 2, yb, size), f32),
            pltpu.VMEM((2 * yb, size), f32),
            pltpu.VMEM((n_row * xb, size), f32),
            pltpu.VMEM((n_row, xb, size), f32),
            dma((16,)),
            dma(()),
            dma((BLOCK_CHUNKS,)),
            dma((n_row,)),
            dma((n_row,)),
            dma((2,)),
            dma((2,)),
            dma((n_row,)),
            dma((n_row,)),
        ],
        compiler_params=pltpu.CompilerParams(
            collective_id=0, has_side_effects=True, vmem_limit_bytes=VMEM_BYTES
        ),
    )(*[a if a.size == 1 else pltpu.with_memory_space_constraint(a, pltpu.HBM) for a in args])
    return hand_out(*results)


def solution(mesh):
    placed = (
        P(("groups", "row"), "col", None, None, None),
        P(("groups", "row"), "col", None),
        P(("groups", "row"), "col", None),
        P(("groups", "row"), "col"),
        P(("groups", "col", "row"), None),
        P(("groups", "col", "row"), None),
        P(("groups", "row", "col"), None),
        P(("groups", "row", "col"), None),
        P(("groups", "col", "row"), None),
        P(("groups", "col", "row"), None),
        P(("groups", "col", "row"), None),
        P(("groups", "col", "row"), None),
        P(("groups", "row", "col"), None),
        P("groups"),
        P("groups"),
    )
    return jax.shard_map(
        functools.partial(body, mesh.shape["row"]),
        mesh=mesh,
        in_specs=placed,
        out_specs=(
            P(("groups", "row", "col"), None),
            P(("groups", "col", "row"), None),
            P(("groups", "col", "row"), None),
        ),
        check_vma=False,
    )
```
